1024 devices in a mesh: wide: 16 (over y, core), narrow: 16 (over z), tp: 4 (over x).
Axes of the slice: x: 4, y: 8, z: 16, core: 2. Of those that a mesh axis runs over, the one named last changes fastest.
Arguments:
- d_out: bfloat16 [4096, 3584], P(('wide', 'narrow')), may hold values from -1.5 to 1.5
- expert_ids: int32 [4096, 8], P(('wide', 'narrow')), may hold values from 0 to 127, as said below
- gate_values: bfloat16 [4096, 8], P(('wide', 'narrow')), may hold values from 0.049804688 to 0.59765625
- stored_preacts: bfloat16 [16, 16, 256, 2, 512], P('wide', 'narrow', None, None, 'tp'), may hold values from -6 to 6
- w_gate: bfloat16 [16, 16, 3584, 512], P('wide', 'narrow', None, 'tp'), may hold values from -0.09375 to 0.09375
- w_up: bfloat16 [16, 16, 3584, 512], P('wide', 'narrow', None, 'tp'), may hold values from -0.09375 to 0.09375
- w_down: bfloat16 [16, 16, 512, 3584], P('wide', 'narrow', 'tp'), may hold values from -0.1875 to 0.1875
Outputs:
- d_tokens: bfloat16 [4096, 3584], P(('wide', 'narrow'), 'tp')
- d_gates: float32 [4096, 8], P(('wide', 'narrow'))
The draws below stay inside these ranges and needn't reach their ends.
Inputs may be any that keep to these rules, and one draw needn't show every extreme that they name: `expert_ids`: each token names 8 distinct experts; expert e lies in group e // 8, and a token's experts lie in exactly 4 groups, 2 in each.
All inputs are finite; a program needn't handle non-finite values.
Results may differ from the reference program's by a relative error of at most 0.017.
Values may be sent and summed in bfloat16 or wider, within the bound.
No kernel may reach another device: no remote copies, remote signals or barrier semaphores. Data moves between devices by JAX's collectives and lax.ppermute only.
A program may use at most 32 MiB of HBM per device.

```python
import jax
import jax.numpy as jnp
from jax import lax

D = 3584
FF = 1024
TOP = 8
LIMIT = 4
HALVES = 2
TOK_DEV = 16
PER_GROUP = 2
GROUPS = 16
EXP_GROUP = 8
EXPERTS = 128
FFH = 512
FFB = 128
TOKENS = 4096
CAP_W = 6
CAP_N = 16
SLOTS = 256
N_WIDE = 16
N_NARROW = 16
N_TP = 4


def draw_expert_ids(key, part):
    key = jax.random.fold_in(key, 17)
    keys = jax.random.split(key, 5)
    group_span = (1 + jax.random.randint(keys[0], (GROUPS,), 0, 8)) * 65536
    expert_span = (1 + jax.random.randint(keys[1], (EXPERTS,), 0, 4)) * 65536
    group_score = jax.random.randint(keys[2], (TOKENS, GROUPS), 0, group_span[None, :])
    group_score = group_score * GROUPS + jnp.arange(GROUPS, dtype=jnp.int32)[None, :]
    chosen = lax.top_k(group_score, LIMIT)[1].astype(jnp.int32)
    expert_score = jax.random.randint(keys[3], (TOKENS, EXPERTS), 0, expert_span[None, :])
    expert_score = expert_score * EXP_GROUP + (jnp.arange(EXPERTS, dtype=jnp.int32) % EXP_GROUP)[None, :]
    grouped = expert_score.reshape(TOKENS, GROUPS, EXP_GROUP)
    inside = jnp.take_along_axis(grouped, jnp.broadcast_to(chosen[:, :, None], (TOKENS, LIMIT, EXP_GROUP)), axis=1)
    picked = lax.top_k(inside, PER_GROUP)[1].astype(jnp.int32)
    named = (chosen[:, :, None] * EXP_GROUP + picked).reshape(TOKENS, TOP)
    shuffle = jax.random.randint(keys[4], (TOKENS, TOP), 0, 1048576) * TOP + jnp.arange(TOP, dtype=jnp.int32)[None, :]
    reorder = jnp.argsort(shuffle, axis=1)
    return jnp.take_along_axis(named, reorder, axis=1).astype(jnp.int32)


def levels(key, extent, cuts, low, largest):
    def one(position, blocks):
        heights = jax.random.uniform(jax.random.fold_in(jax.random.fold_in(key, 6), position), (blocks,), jnp.float32, low / len(cuts), largest / len(cuts))
        return jnp.repeat(jnp.exp(heights), extent[position] // blocks).reshape((-1,) + (1,) * (len(extent) - position - 1))

    loudness = one(*cuts[0])
    for cut in cuts[1:]:
        loudness = loudness * one(*cut)
    return loudness


def noise(key, extent, scale, reach, pieces=(), kind=jnp.bfloat16):
    entries = scale * jax.random.normal(key, extent, jnp.float32)
    if pieces:
        entries = entries * levels(key, extent, pieces, -0.22, 0.18)
    return jnp.clip(entries, -reach, reach).astype(kind)


def setup_inputs(seed: int = 0) -> dict:
    key_of = jax.random.split(jax.random.key(seed), 8)
    return {
        "d_out": noise(key_of[0], (TOKENS, D), 0.25, 1.5, ((0, 256),)),
        "expert_ids": draw_expert_ids(jax.random.fold_in(key_of[7], 71), 0),
        "gate_values": jnp.clip(0.049804688 + 0.54785156 * jax.random.uniform(key_of[2], (TOKENS, TOP), jnp.float32) ** levels(key_of[2], (TOKENS, TOP), ((0, 256),), -0.2, 0.2), 0.049804688, 0.59765625).astype(jnp.bfloat16),
        "stored_preacts": noise(key_of[3], (GROUPS, HALVES * EXP_GROUP, SLOTS, 2, FFH), 1.0, 6.0, ((0, 16), (1, 16), (4, 4))),
        "w_gate": noise(key_of[4], (GROUPS, HALVES * EXP_GROUP, D, FFH), D ** -0.5, 0.09375, ((0, 16), (1, 16), (3, 4))),
        "w_up": noise(key_of[5], (GROUPS, HALVES * EXP_GROUP, D, FFH), D ** -0.5, 0.09375, ((0, 16), (1, 16), (3, 4))),
        "w_down": noise(key_of[6], (GROUPS, HALVES * EXP_GROUP, FFH, D), FF ** -0.5, 0.1875, ((0, 16), (1, 16), (2, 4))),
    }


def swish_parts(gate_pre):
    sigmoid_value = jax.nn.sigmoid(gate_pre)
    swish_value = gate_pre * sigmoid_value
    return swish_value, sigmoid_value * (1.0 + gate_pre * (1.0 - sigmoid_value))


def route_tables(expert_ids):
    token_group = expert_ids // EXP_GROUP
    member = jnp.max((token_group[:, :, None] == jnp.arange(GROUPS, dtype=jnp.int32)[None, None, :]).astype(jnp.int32), axis=1)
    blocked = member.reshape(TOKENS // TOK_DEV, TOK_DEV, GROUPS)
    first_rank = (jnp.cumsum(blocked, axis=1) - blocked).reshape(TOKENS, GROUPS)
    first_keep = (member > 0) & (first_rank < CAP_W)
    route_keep = jnp.take_along_axis(first_keep, token_group, axis=1)
    expert_hit = (expert_ids[:, :, None] == jnp.arange(EXPERTS, dtype=jnp.int32)[None, None, :]) & route_keep[:, :, None]
    hit_count = jnp.sum(expert_hit.astype(jnp.int32), axis=1)
    arranged = hit_count.reshape(N_WIDE, N_NARROW, TOK_DEV, EXPERTS).transpose(1, 0, 2, 3).reshape(N_NARROW, N_WIDE * TOK_DEV, EXPERTS)
    ranked = jnp.cumsum(arranged, axis=1) - arranged
    second_all = ranked.reshape(N_NARROW, N_WIDE, TOK_DEV, EXPERTS).transpose(1, 0, 2, 3).reshape(TOKENS, EXPERTS)
    second_rank = jnp.take_along_axis(second_all, expert_ids, axis=1)
    route_kept = route_keep & (second_rank < CAP_N)
    source_lane = (jnp.arange(TOKENS, dtype=jnp.int32) // TOK_DEV) % N_NARROW
    slot_index = source_lane[:, None] * CAP_N + second_rank
    return route_kept, slot_index


def expert_terms(expert_index, slot_rows, slot_scale, stored_preacts, w_gate, w_up, w_down):
    group_index = expert_index // EXP_GROUP
    lane_index = expert_index % EXP_GROUP
    input_total = jnp.zeros((SLOTS, D), jnp.float32)
    score_total = jnp.zeros((SLOTS,), jnp.float32)
    for half_index in range(HALVES):
        column = half_index * EXP_GROUP + lane_index
        gate_pre = stored_preacts[group_index, column, :, 0, :].astype(jnp.float32)
        up_pre = stored_preacts[group_index, column, :, 1, :].astype(jnp.float32)
        gate_one = w_gate[group_index, column]
        up_one = w_up[group_index, column]
        down_one = w_down[group_index, column]
        back_proj = jnp.dot(slot_rows, down_one.T, preferred_element_type=jnp.float32)
        swish_value, swish_slope = swish_parts(gate_pre)
        hidden = swish_value * up_pre
        block_scores = jnp.sum((hidden * back_proj).reshape(SLOTS, N_TP, FFB), axis=2)
        score_total = score_total + jnp.sum(lax.optimization_barrier(block_scores.astype(jnp.bfloat16)).astype(jnp.float32), axis=1)
        hidden_grad = slot_scale[:, None] * back_proj
        grad_gate = (hidden_grad * up_pre * swish_slope).astype(jnp.bfloat16)
        grad_up = (hidden_grad * swish_value).astype(jnp.bfloat16)
        block_inputs = jnp.einsum("sqf,dqf->sqd", grad_gate.reshape(SLOTS, N_TP, FFB).astype(jnp.float32), gate_one.reshape(D, N_TP, FFB).astype(jnp.float32), precision=lax.Precision.HIGHEST)
        block_inputs = block_inputs + jnp.einsum("sqf,dqf->sqd", grad_up.reshape(SLOTS, N_TP, FFB).astype(jnp.float32), up_one.reshape(D, N_TP, FFB).astype(jnp.float32), precision=lax.Precision.HIGHEST)
        input_total = input_total + jnp.sum(lax.optimization_barrier(block_inputs.astype(jnp.bfloat16)).astype(jnp.float32), axis=1)
    return input_total, score_total


def reference(d_out, expert_ids, gate_values, stored_preacts, w_gate, w_up, w_down):
    route_kept, slot_index = route_tables(expert_ids)
    target = jnp.where(route_kept, slot_index, SLOTS).astype(jnp.int32)
    token_of = jnp.broadcast_to(jnp.arange(TOKENS, dtype=jnp.int32)[:, None], (TOKENS, TOP))
    slot_token = jnp.full((EXPERTS, SLOTS), TOKENS, jnp.int32).at[expert_ids, target].set(token_of, mode="drop")
    slot_gate = jnp.zeros((EXPERTS, SLOTS), jnp.float32).at[expert_ids, target].set(gate_values.astype(jnp.float32), mode="drop")
    padded = jnp.concatenate([d_out, jnp.zeros((1, D), d_out.dtype)], axis=0)

    def add_expert(grad_total, expert_index):
        slot_rows = jnp.take(padded, slot_token[expert_index], axis=0)
        input_rows, score_rows = expert_terms(expert_index, slot_rows, slot_gate[expert_index], stored_preacts, w_gate, w_up, w_down)
        return grad_total.at[slot_token[expert_index]].add(input_rows), score_rows

    grad_total, score_all = lax.scan(add_expert, jnp.zeros((TOKENS + 1, D), jnp.float32), jnp.arange(EXPERTS, dtype=jnp.int32))
    d_tokens = grad_total[:TOKENS].astype(jnp.bfloat16)
    safe_slot = jnp.minimum(slot_index, SLOTS - 1).astype(jnp.int32)
    d_gates = jnp.where(route_kept, score_all[expert_ids, safe_slot], jnp.zeros((), jnp.float32))
    return d_tokens, d_gates
```

```python
import jax
import jax.numpy as jnp
from jax import lax
from jax.experimental import pallas as pl
from jax.experimental.pallas import tpu as pltpu
from jax.sharding import PartitionSpec as P

LIMIT = 4
HALVES = 2
BLOCK = 8
TILE = 128


def nn(left, right):
    return lax.dot_general(
        left, right, (((1,), (0,)), ((), ())), preferred_element_type=jnp.float32
    )


def nt(left, right):
    return lax.dot_general(
        left, right, (((1,), (1,)), ((), ())), preferred_element_type=jnp.float32
    )


def iota(shape, axis):
    return lax.broadcasted_iota(jnp.int32, shape, axis)


def bits(mask):
    return jnp.where(mask, 1.0, 0.0).astype(jnp.bfloat16)


def call(kernel, outs, args, flops=0, size=1 << 20):
    return pl.pallas_call(
        kernel,
        out_shape=outs,
        in_specs=[pl.BlockSpec(memory_space=pltpu.VMEM)] * len(args),
        out_specs=jax.tree.map(lambda _: pl.BlockSpec(memory_space=pltpu.VMEM), outs),
        compiler_params=pltpu.CompilerParams(vmem_limit_bytes=40 << 20),
        cost_estimate=pl.CostEstimate(flops=flops, bytes_accessed=size, transcendentals=0),
    )(*args)


def shape(*dims, dtype=jnp.bfloat16):
    return jax.ShapeDtypeStruct(dims, dtype)


def pack_down_kernel(down_ref, *refs):
    out_refs, ready_ref = refs[:-1], refs[-1]
    ready_ref[...] = jnp.zeros_like(ready_ref)
    count = len(out_refs)
    width = down_ref.shape[1] // count
    me = lax.axis_index("tp")
    for step, out_ref in enumerate(out_refs):
        to = lax.rem(me + step, count)
        out_ref[...] = down_ref[:, pl.ds(pl.multiple_of(to * width, TILE), width)]


def pack_rest_kernel(gate_ref, up_ref, preact_ref, *refs):
    out_refs, ready_ref = refs[:-1], refs[-1]
    ready_ref[...] = jnp.zeros_like(ready_ref)
    count = len(out_refs)
    width = gate_ref.shape[0] // count
    me = lax.axis_index("tp")
    for step, out_ref in enumerate(out_refs):
        to = lax.rem(me + step, count)
        rows = pl.ds(pl.multiple_of(to * width, TILE), width)
        out_ref[0:width, :] = gate_ref[rows, :]
        out_ref[width : 2 * width, :] = up_ref[rows, :]
        out_ref[2 * width :, :] = preact_ref[...]


def spread(group_cap, rows):
    r, c = iota((rows, rows), 0), iota((rows, rows), 1)
    return bits((r // BLOCK == c // BLOCK) & (r % BLOCK == group_cap))


def collect(group_cap, rows):
    r, c = iota((rows, rows), 0), iota((rows, rows), 1)
    return bits(
        (r // BLOCK == c // BLOCK) & (c % BLOCK == group_cap) & (r % BLOCK < group_cap)
    )


def own_span(rows, width):
    r, c = iota((rows, rows), 0), iota((rows, rows), 1)
    return c // width == r % BLOCK


def first_kernel(group_cap, width, ids_ref, gates_ref, rows_ref, ready_ref, send_ref, place_ref):
    top, tokens = ids_ref.shape
    rows = send_ref.shape[0]
    groups = rows // BLOCK
    columns = send_ref.shape[1]
    ids = ids_ref[...]
    gates = gates_ref[...].astype(jnp.float32)
    member = jnp.zeros((groups, tokens), jnp.float32)
    table = jnp.zeros((groups * width, tokens), jnp.float32)
    for k in range(top):
        one = ids[k : k + 1, :]
        member = jnp.where(one // width == iota((groups, tokens), 0), 1.0, member)
        table = jnp.where(one == iota((groups * width, tokens), 0), gates[k : k + 1, :], table)
    earlier = bits(iota((tokens, tokens), 0) < iota((tokens, tokens), 1))
    rank = nn(member.astype(jnp.bfloat16), earlier)
    rank = jnp.where((member > 0) & (rank < group_cap), rank, 100.0)
    grow = bits(iota((rows, groups), 0) // BLOCK == iota((rows, groups), 1))
    place = nn(grow, rank.astype(jnp.bfloat16)) == (
        iota((rows, tokens), 0) % BLOCK
    ).astype(jnp.float32)
    place = bits(place)
    place_ref[...] = place
    columns_at = pl.ds(pl.multiple_of(lax.axis_index("tp") * columns, TILE), columns)
    send_ref[...] = nn(place, rows_ref[:, columns_at]).astype(jnp.bfloat16)
    r, c = iota((rows, groups * width), 0), iota((rows, groups * width), 1)
    paired = nt(place, table.astype(jnp.bfloat16))
    paired = jnp.where(r // BLOCK == c // width, paired, 0.0).astype(jnp.bfloat16)
    a, b = iota((groups * width, rows), 0), iota((groups * width, rows), 1)
    repeated = nn(paired, bits(a % width == b % width))
    repeated = jnp.where(own_span(rows, width), repeated, 0.0).astype(jnp.bfloat16)
    notes = nn(spread(group_cap, rows), repeated)
    first = send_ref[:, 0:rows].astype(jnp.float32)
    send_ref[:, 0:rows] = (first + notes).astype(jnp.bfloat16)


def second_kernel(group_cap, width, lane_cap, got_ref, *refs):
    out_ref, gated_ref = refs[-2:]
    rows = got_ref.shape[0]
    got = got_ref[...]
    notes = nn(collect(group_cap, rows), got[:, 0:rows])
    notes = jnp.where(own_span(rows, width), notes, 0.0).astype(jnp.bfloat16)
    slots = width * lane_cap
    a, b = iota((rows, slots), 0), iota((rows, slots), 1)
    gate = nn(notes, bits((a % width == b // lane_cap) & (a < group_cap * width)))
    hit = gate != 0.0
    rank = nn(bits(iota((rows, rows), 1) < iota((rows, rows), 0)), bits(hit))
    place = hit & (rank == (b % lane_cap).astype(jnp.float32))
    gated_ref[...] = jnp.where(place, gate, 0.0).astype(jnp.bfloat16)
    turned = jnp.transpose(jnp.where(place, 1.0, 0.0)).astype(jnp.bfloat16)
    moved = nn(turned, got).astype(jnp.bfloat16)
    for half in range(HALVES):
        out_ref[half] = moved


def partial_kernel(rows_ref, *refs):
    out_ref = refs[-1]
    rows = rows_ref[...]
    blocks = [block_ref[...] for block_ref in refs[:-1]]
    out_ref[...] = nt(rows, jnp.concatenate(blocks, axis=0)).astype(jnp.bfloat16)


def cycle_sum(terms):
    count = len(terms)
    while count > 1:
        count //= 2
        terms = [terms[i] + terms[i + count] for i in range(count)]
    return terms[0]


def expert_kernel(count, *refs):
    parts, blocks, out_ref = refs[:count], refs[count : 2 * count], refs[-1]
    slots = out_ref.shape[0]
    columns = out_ref.shape[1] - TILE
    hidden = parts[0].shape[1] // count
    grads, weights, scores = [], [], []
    for at in range(count):
        pieces = []
        for step in range(count):
            source = (at - step) % count
            pieces.append(
                parts[step][:, source * hidden : (source + 1) * hidden].astype(jnp.float32)
            )
        back = cycle_sum(pieces)
        gate_pre = blocks[at][2 * columns : 2 * columns + slots, :].astype(jnp.float32)
        up_pre = blocks[at][2 * columns + slots :, :].astype(jnp.float32)
        sigmoid_value = jax.nn.sigmoid(gate_pre)
        swish_value = gate_pre * sigmoid_value
        slope = sigmoid_value * (1.0 + gate_pre * (1.0 - sigmoid_value))
        up_part = swish_value * back
        scores.append(up_part * up_pre)
        grads.append((back * up_pre * slope).astype(jnp.bfloat16))
        grads.append(up_part.astype(jnp.bfloat16))
        weights.append(blocks[at][0:columns, :])
        weights.append(blocks[at][columns : 2 * columns, :])
    total = nt(jnp.concatenate(grads, axis=1), jnp.concatenate(weights, axis=1))
    out_ref[:, 0:columns] = total.astype(jnp.bfloat16)
    score = jnp.sum(cycle_sum(scores), axis=1, keepdims=True)
    out_ref[:, columns:] = jnp.broadcast_to(score, (slots, TILE)).astype(jnp.bfloat16)


def rows_kernel(group_cap, width, lane_cap, gated_ref, back_ref, out_ref):
    rows, columns = out_ref.shape
    gated = gated_ref[...]
    both = jnp.concatenate([gated, gated], axis=1)
    out_ref[...] = nn(both, back_ref[:, 0:columns]).astype(jnp.bfloat16)
    place = bits(both != 0)
    slots = both.shape[1]
    a, b = iota((slots, TILE), 0), iota((slots, TILE), 1)
    score = back_ref[:, columns:].astype(jnp.float32)
    score = jnp.where((a // lane_cap) % width == b % width, score, 0.0).astype(jnp.bfloat16)
    score = nn(place, score)
    score = jnp.where(own_span(rows, width), score, 0.0).astype(jnp.bfloat16)
    notes = nn(spread(group_cap, rows), score)
    first = out_ref[:, 0:rows].astype(jnp.float32)
    out_ref[:, 0:rows] = (first + notes).astype(jnp.bfloat16)


def last_kernel(group_cap, width, ids_ref, place_ref, home_ref, tokens_ref, gates_ref):
    top, tokens = ids_ref.shape
    rows = home_ref.shape[0]
    ids = ids_ref[...]
    home = home_ref[...]
    place = jnp.transpose(place_ref[...].astype(jnp.float32)).astype(jnp.bfloat16)
    tokens_ref[...] = nn(place, home).astype(jnp.bfloat16)
    notes = nn(collect(group_cap, rows), home[:, 0:rows])
    notes = jnp.where(own_span(rows, width), notes, 0.0).astype(jnp.bfloat16)
    a, b = iota((rows, rows), 0), iota((rows, rows), 1)
    wide = nn(notes, bits((a % width == b % width) & (a < group_cap * width)))
    wide = jnp.where(a // BLOCK == b // width, wide, 0.0).astype(jnp.bfloat16)
    score = jnp.transpose(nn(place, wide))
    at = iota((rows, tokens), 0)
    for k in range(top):
        gates_ref[k : k + 1, :] = jnp.sum(
            jnp.where(ids[k : k + 1, :] == at, score, 0.0), axis=0, keepdims=True
        )


def exchange(values, axis):
    return lax.all_to_all(values, axis, split_axis=0, concat_axis=0, tiled=True)


def shift(values, step, count):
    return lax.ppermute(
        values, "tp", [(source, (source + step) % count) for source in range(count)]
    )


def per_device(d_out, expert_ids, gate_values, stored_preacts, w_gate, w_up, w_down):
    wide_count = lax.axis_size("wide")
    lane_count = lax.axis_size("narrow")
    split_count = lax.axis_size("tp")
    group_width = lane_count // HALVES
    token_count, model_width = d_out.shape
    slot_count = stored_preacts.shape[2]
    hidden_width = stored_preacts.shape[4]
    lane_cap = slot_count // lane_count
    group_cap = min(token_count, max(1, 3 * token_count * LIMIT // (2 * wide_count)))
    columns = model_width // split_count
    rows = wide_count * BLOCK
    lanes = group_width * lane_cap
    ids = expert_ids.T

    down_packed = call(
        pack_down_kernel,
        [shape(hidden_width, columns)] * split_count + [shape(BLOCK, TILE)],
        (w_down[0, 0],),
    )
    downs = [down_packed[0]] + [
        shift(down_packed[step], step, split_count) for step in range(1, split_count)
    ]
    rest_packed = call(
        pack_rest_kernel,
        [shape(2 * columns + 2 * slot_count, hidden_width)] * split_count + [shape(BLOCK, TILE)],
        (
            w_gate[0, 0],
            w_up[0, 0],
            stored_preacts[0, 0].transpose(1, 0, 2).reshape(2 * slot_count, hidden_width),
        ),
        size=4 << 20,
    )
    blocks = [rest_packed[0]] + [
        shift(rest_packed[step], step, split_count) for step in range(1, split_count)
    ]

    send, place = call(
        lambda *refs: first_kernel(group_cap, group_width, *refs),
        [shape(rows, columns), shape(rows, token_count)],
        (ids, gate_values.T, d_out, down_packed[-1]),
    )
    got = exchange(send.reshape(wide_count, BLOCK, columns), "wide").reshape(rows, columns)
    forward, gated = call(
        lambda *refs: second_kernel(group_cap, group_width, lane_cap, *refs),
        [shape(HALVES, lanes, columns), shape(rows, lanes)],
        (got, rest_packed[-1], *downs[1:]),
    )
    slot_rows = exchange(forward.reshape(lane_count, lane_cap, columns), "narrow").reshape(
        slot_count, columns
    )
    partial = call(
        partial_kernel,
        shape(slot_count, split_count * hidden_width),
        (slot_rows, *downs),
    )
    parts = [partial] + [shift(partial, step, split_count) for step in range(1, split_count)]
    terms = call(
        lambda *refs: expert_kernel(split_count, *refs),
        shape(slot_count, columns + TILE),
        (*parts, *blocks),
    )
    back = exchange(terms.reshape(lane_count, lane_cap, columns + TILE), "narrow").reshape(
        slot_count, columns + TILE
    )
    row_input = call(
        lambda *refs: rows_kernel(group_cap, group_width, lane_cap, *refs),
        shape(rows, columns),
        (gated, back),
    )
    home = exchange(row_input.reshape(wide_count, BLOCK, columns), "wide").reshape(rows, columns)
    d_tokens, d_gates = call(
        lambda *refs: last_kernel(group_cap, group_width, *refs),
        [
            shape(token_count, columns),
            shape(expert_ids.shape[1], token_count, dtype=jnp.float32),
        ],
        (ids, place, home),
    )
    return (d_tokens, d_gates.T)


def solution(mesh):
    return jax.shard_map(
        per_device,
        mesh=mesh,
        in_specs=(
            P(("wide", "narrow"), None),
            P(("wide", "narrow"), None),
            P(("wide", "narrow"), None),
            P("wide", "narrow", None, None, "tp"),
            P("wide", "narrow", None, "tp"),
            P("wide", "narrow", None, "tp"),
            P("wide", "narrow", "tp", None),
        ),
        out_specs=(P(("wide", "narrow"), "tp"), P(("wide", "narrow"), None)),
        check_vma=False,
    )
```

```python
import jax
import jax.numpy as jnp
from jax import lax
from jax.experimental import pallas as pl
from jax.experimental.pallas import tpu as pltpu
from jax.sharding import PartitionSpec as P

LIMIT = 4
HALVES = 2
BLOCK = 8
TILE = 128


def nn(left, right):
    return lax.dot_general(
        left, right, (((1,), (0,)), ((), ())), preferred_element_type=jnp.float32
    )


def nt(left, right):
    return lax.dot_general(
        left, right, (((1,), (1,)), ((), ())), preferred_element_type=jnp.float32
    )


def iota(shape, axis):
    return lax.broadcasted_iota(jnp.int32, shape, axis)


def bits(mask):
    return jnp.where(mask, 1.0, 0.0).astype(jnp.bfloat16)


def call(kernel, outs, args, flops=0, size=1 << 20, spaces=None, scratch=(), vmem=16):
    spaces = spaces or [pltpu.VMEM] * len(args)
    return pl.pallas_call(
        kernel,
        out_shape=outs,
        in_specs=[pl.BlockSpec(memory_space=space) for space in spaces],
        out_specs=jax.tree.map(lambda _: pl.BlockSpec(memory_space=pltpu.VMEM), outs),
        scratch_shapes=list(scratch),
        compiler_params=pltpu.CompilerParams(vmem_limit_bytes=vmem << 20),
        cost_estimate=pl.CostEstimate(flops=flops, bytes_accessed=size, transcendentals=0),
    )(*args)


def shape(*dims, dtype=jnp.bfloat16):
    return jax.ShapeDtypeStruct(dims, dtype)


def pack_down_kernel(steps, count, down_ref, after_ref, *out_refs):
    width = down_ref.shape[1] // count
    me = lax.axis_index("tp")
    for step, out_ref in zip(steps, out_refs):
        to = lax.rem(me + step, count)
        out_ref[...] = down_ref[:, pl.ds(pl.multiple_of(to * width, TILE), width)]


def pack_rest_kernel(gate_ref, up_ref, down_ref, *refs):
    out_refs, ready_ref = refs[:-1], refs[-1]
    ready_ref[...] = jnp.zeros_like(ready_ref)
    count = len(out_refs)
    width, hidden = gate_ref.shape[0] // count, gate_ref.shape[1]
    me = lax.axis_index("tp")
    for step, out_ref in enumerate(out_refs):
        to = lax.rem(me + step, count)
        rows = pl.ds(pl.multiple_of(to * width, TILE), width)
        out_ref[0:width, :] = gate_ref[rows, :]
        out_ref[width : 2 * width, :] = up_ref[rows, :]
        if out_ref.shape[0] > 2 * width:
            for tile in range(width // TILE):
                lanes = pl.ds(pl.multiple_of(to * width + tile * TILE, TILE), TILE)
                first = 2 * width + tile * hidden
                out_ref[first : first + hidden, :] = down_ref[:, lanes]


def spread(group_cap, rows):
    r, c = iota((rows, rows), 0), iota((rows, rows), 1)
    return bits((r // BLOCK == c // BLOCK) & (r % BLOCK == group_cap))


def collect(group_cap, rows):
    r, c = iota((rows, rows), 0), iota((rows, rows), 1)
    return bits(
        (r // BLOCK == c // BLOCK) & (c % BLOCK == group_cap) & (r % BLOCK < group_cap)
    )


def own_span(rows, width):
    r, c = iota((rows, rows), 0), iota((rows, rows), 1)
    return c // width == r % BLOCK


def first_kernel(
    group_cap, width, ids_hbm, gates_hbm, rows_hbm, send_ref, place_ref, ids_ref, gates_ref, rows_ref, sems
):
    columns = send_ref.shape[1]
    columns_at = pl.ds(pl.multiple_of(lax.axis_index("tp") * columns, TILE), columns)
    copies = [
        pltpu.make_async_copy(ids_hbm, ids_ref, sems.at[0]),
        pltpu.make_async_copy(gates_hbm, gates_ref, sems.at[1]),
        pltpu.make_async_copy(rows_hbm.at[:, columns_at], rows_ref, sems.at[2]),
    ]
    for copy in copies:
        copy.start()
    for copy in copies:
        copy.wait()
    top, tokens = ids_ref.shape
    rows = send_ref.shape[0]
    groups = rows // BLOCK
    ids = ids_ref[...]
    gates = gates_ref[...].astype(jnp.float32)
    member = jnp.zeros((groups, tokens), jnp.float32)
    table = jnp.zeros((groups * width, tokens), jnp.float32)
    for k in range(top):
        one = ids[k : k + 1, :]
        member = jnp.where(one // width == iota((groups, tokens), 0), 1.0, member)
        table = jnp.where(one == iota((groups * width, tokens), 0), gates[k : k + 1, :], table)
    earlier = bits(iota((tokens, tokens), 0) < iota((tokens, tokens), 1))
    rank = nn(member.astype(jnp.bfloat16), earlier)
    rank = jnp.where((member > 0) & (rank < group_cap), rank, 100.0)
    grow = bits(iota((rows, groups), 0) // BLOCK == iota((rows, groups), 1))
    place = nn(grow, rank.astype(jnp.bfloat16)) == (
        iota((rows, tokens), 0) % BLOCK
    ).astype(jnp.float32)
    place = bits(place)
    place_ref[...] = place
    send_ref[...] = nn(place, rows_ref[...]).astype(jnp.bfloat16)
    r, c = iota((rows, groups * width), 0), iota((rows, groups * width), 1)
    paired = nt(place, table.astype(jnp.bfloat16))
    paired = jnp.where(r // BLOCK == c // width, paired, 0.0).astype(jnp.bfloat16)
    a, b = iota((groups * width, rows), 0), iota((groups * width, rows), 1)
    repeated = nn(paired, bits(a % width == b % width))
    repeated = jnp.where(own_span(rows, width), repeated, 0.0).astype(jnp.bfloat16)
    notes = nn(spread(group_cap, rows), repeated)
    first = send_ref[:, 0:rows].astype(jnp.float32)
    send_ref[:, 0:rows] = (first + notes).astype(jnp.bfloat16)


def second_kernel(group_cap, width, lane_cap, got_ref, *refs):
    out_ref, gated_ref = refs[-2:]
    rows = got_ref.shape[0]
    got = got_ref[...]
    notes = nn(collect(group_cap, rows), got[:, 0:rows])
    notes = jnp.where(own_span(rows, width), notes, 0.0).astype(jnp.bfloat16)
    slots = width * lane_cap
    a, b = iota((rows, slots), 0), iota((rows, slots), 1)
    gate = nn(notes, bits((a % width == b // lane_cap) & (a < group_cap * width)))
    hit = gate != 0.0
    rank = nn(bits(iota((rows, rows), 1) < iota((rows, rows), 0)), bits(hit))
    place = hit & (rank == (b % lane_cap).astype(jnp.float32))
    gated_ref[...] = jnp.where(place, gate, 0.0).astype(jnp.bfloat16)
    turned = jnp.transpose(jnp.where(place, 1.0, 0.0)).astype(jnp.bfloat16)
    moved = nn(turned, got).astype(jnp.bfloat16)
    for half in range(HALVES):
        out_ref[half] = moved


def partial_kernel(rows_ref, *refs):
    refs, out_ref = refs[:-2], refs[-1]
    rows = rows_ref[...]
    columns = rows_ref.shape[1]
    blocks = []
    for block_ref in refs:
        if block_ref.shape[1] == columns:
            blocks.append(block_ref[...])
            continue
        hidden = (block_ref.shape[0] - 2 * columns) * TILE // columns
        firsts = [2 * columns + tile * hidden for tile in range(columns // TILE)]
        blocks.append(
            jnp.concatenate([block_ref[first : first + hidden, :] for first in firsts], axis=1)
        )
    out_ref[...] = nt(rows, jnp.concatenate(blocks, axis=0)).astype(jnp.bfloat16)


def cycle_sum(terms):
    count = len(terms)
    while count > 1:
        count //= 2
        terms = [terms[i] + terms[i + count] for i in range(count)]
    return terms[0]


def expert_kernel(count, *refs):
    parts, blocks, preacts_ref, out_ref = refs[:count], refs[count : 2 * count], *refs[-2:]
    me = lax.axis_index("tp")
    slots = out_ref.shape[0]
    columns = out_ref.shape[1] - TILE
    hidden = parts[0].shape[1] // count
    grads, weights, scores = [], [], []
    for at in range(count):
        pieces = []
        for step in range(count):
            source = (at - step) % count
            pieces.append(
                parts[step][:, source * hidden : (source + 1) * hidden].astype(jnp.float32)
            )
        back = cycle_sum(pieces)
        block = lax.rem(me + count - at, count)
        gate_pre = preacts_ref[block, 0:slots, :].astype(jnp.float32)
        up_pre = preacts_ref[block, slots : 2 * slots, :].astype(jnp.float32)
        sigmoid_value = jax.nn.sigmoid(gate_pre)
        swish_value = gate_pre * sigmoid_value
        slope = sigmoid_value * (1.0 + gate_pre * (1.0 - sigmoid_value))
        up_part = swish_value * back
        scores.append(up_part * up_pre)
        grads.append((back * up_pre * slope).astype(jnp.bfloat16))
        grads.append(up_part.astype(jnp.bfloat16))
        weights.append(blocks[at][0:columns, :])
        weights.append(blocks[at][columns : 2 * columns, :])
    total = nt(jnp.concatenate(grads, axis=1), jnp.concatenate(weights, axis=1))
    out_ref[:, 0:columns] = total.astype(jnp.bfloat16)
    score = jnp.sum(cycle_sum(scores), axis=1, keepdims=True)
    out_ref[:, columns:] = jnp.broadcast_to(score, (slots, TILE)).astype(jnp.bfloat16)


def rows_kernel(group_cap, width, lane_cap, gated_ref, back_ref, out_ref):
    rows, columns = out_ref.shape
    gated = gated_ref[...]
    both = jnp.concatenate([gated, gated], axis=1)
    out_ref[...] = nn(both, back_ref[:, 0:columns]).astype(jnp.bfloat16)
    place = bits(both != 0)
    slots = both.shape[1]
    a, b = iota((slots, TILE), 0), iota((slots, TILE), 1)
    score = back_ref[:, columns:].astype(jnp.float32)
    score = jnp.where((a // lane_cap) % width == b % width, score, 0.0).astype(jnp.bfloat16)
    score = nn(place, score)
    score = jnp.where(own_span(rows, width), score, 0.0).astype(jnp.bfloat16)
    notes = nn(spread(group_cap, rows), score)
    first = out_ref[:, 0:rows].astype(jnp.float32)
    out_ref[:, 0:rows] = (first + notes).astype(jnp.bfloat16)


def last_kernel(group_cap, width, ids_ref, place_ref, home_ref, tokens_ref, gates_ref):
    top, tokens = ids_ref.shape
    rows = home_ref.shape[0]
    ids = ids_ref[...]
    home = home_ref[...]
    place = jnp.transpose(place_ref[...].astype(jnp.float32)).astype(jnp.bfloat16)
    tokens_ref[...] = nn(place, home).astype(jnp.bfloat16)
    notes = nn(collect(group_cap, rows), home[:, 0:rows])
    notes = jnp.where(own_span(rows, width), notes, 0.0).astype(jnp.bfloat16)
    a, b = iota((rows, rows), 0), iota((rows, rows), 1)
    wide = nn(notes, bits((a % width == b % width) & (a < group_cap * width)))
    wide = jnp.where(a // BLOCK == b // width, wide, 0.0).astype(jnp.bfloat16)
    score = jnp.transpose(nn(place, wide))
    at = iota((rows, tokens), 0)
    for k in range(top):
        gates_ref[k : k + 1, :] = jnp.sum(
            jnp.where(ids[k : k + 1, :] == at, score, 0.0), axis=0, keepdims=True
        )


def exchange(values, axis):
    return lax.all_to_all(values, axis, split_axis=0, concat_axis=0, tiled=True)


def shift(values, step, count):
    return lax.ppermute(
        values, "tp", [(source, (source + step) % count) for source in range(count)]
    )


def shift_all(values):
    count = len(values)
    order = sorted(range(1, count), key=lambda step: min(step, count - step))
    moved = {step: shift(values[step], step, count) for step in order}
    return [values[0]] + [moved[step] for step in range(1, count)]


def per_device(d_out, expert_ids, gate_values, stored_preacts, w_gate, w_up, w_down):
    wide_count = lax.axis_size("wide")
    lane_count = lax.axis_size("narrow")
    split_count = lax.axis_size("tp")
    group_width = lane_count // HALVES
    token_count, model_width = d_out.shape
    slot_count = stored_preacts.shape[2]
    hidden_width = stored_preacts.shape[4]
    lane_cap = slot_count // lane_count
    group_cap = min(token_count, max(1, 3 * token_count * LIMIT // (2 * wide_count)))
    columns = model_width // split_count
    rows = wide_count * BLOCK
    lanes = group_width * lane_cap
    ids = expert_ids.T

    send, place = call(
        lambda *refs: first_kernel(group_cap, group_width, *refs),
        [shape(rows, columns), shape(rows, token_count)],
        (ids, gate_values.T, d_out),
        spaces=[pltpu.HBM] * 3,
        vmem=60,
        scratch=[
            pltpu.VMEM(ids.shape, ids.dtype),
            pltpu.VMEM(ids.shape, gate_values.dtype),
            pltpu.VMEM((token_count, columns), d_out.dtype),
            pltpu.SemaphoreType.DMA((3,)),
        ],
    )
    half = split_count // 2
    steps = [step for step in range(split_count) if step != half]
    down_packed = call(
        lambda *refs: pack_down_kernel(steps, split_count, *refs),
        [shape(hidden_width, columns)] * len(steps),
        (w_down[0, 0], place),
        spaces=[pltpu.VMEM, pl.ANY],
    )
    downs = {
        step: shift(block, step, split_count) if step else block
        for step, block in zip(steps, down_packed)
    }
    sizes = [(3 if step == half else 2) * columns for step in range(split_count)]
    rest_packed = call(
        pack_rest_kernel,
        [shape(size, hidden_width) for size in sizes] + [shape(BLOCK, TILE)],
        (w_gate[0, 0], w_up[0, 0], w_down[0, 0]),
        size=4 << 20,
    )
    blocks = shift_all(rest_packed[:-1])
    downs[half] = blocks[half]
    preacts = lax.all_gather(
        stored_preacts[0, 0].transpose(1, 0, 2).reshape(2 * slot_count, hidden_width), "tp"
    )

    got = exchange(send.reshape(wide_count, BLOCK, columns), "wide").reshape(rows, columns)
    forward, gated = call(
        lambda *refs: second_kernel(group_cap, group_width, lane_cap, *refs),
        [shape(HALVES, lanes, columns), shape(rows, lanes)],
        (got, rest_packed[-1], downs[1], downs[split_count - 1]),
        spaces=[pltpu.VMEM] + [pl.ANY] * 3,
    )
    slot_rows = exchange(forward.reshape(lane_count, lane_cap, columns), "narrow").reshape(
        slot_count, columns
    )
    partial = call(
        partial_kernel,
        shape(slot_count, split_count * hidden_width),
        (slot_rows, *(downs[step] for step in range(split_count)), preacts),
        spaces=[pltpu.VMEM] * (split_count + 1) + [pl.ANY],
    )
    parts = shift_all([partial] * split_count)
    terms = call(
        lambda *refs: expert_kernel(split_count, *refs),
        shape(slot_count, columns + TILE),
        (*parts, *blocks, preacts),
        vmem=24,
    )
    back = exchange(terms.reshape(lane_count, lane_cap, columns + TILE), "narrow").reshape(
        slot_count, columns + TILE
    )
    row_input = call(
        lambda *refs: rows_kernel(group_cap, group_width, lane_cap, *refs),
        shape(rows, columns),
        (gated, back),
    )
    home = exchange(row_input.reshape(wide_count, BLOCK, columns), "wide").reshape(rows, columns)
    d_tokens, d_gates = call(
        lambda *refs: last_kernel(group_cap, group_width, *refs),
        [
            shape(token_count, columns),
            shape(expert_ids.shape[1], token_count, dtype=jnp.float32),
        ],
        (ids, place, home),
    )
    return (d_tokens, d_gates.T)


def solution(mesh):
    return jax.shard_map(
        per_device,
        mesh=mesh,
        in_specs=(
            P(("wide", "narrow"), None),
            P(("wide", "narrow"), None),
            P(("wide", "narrow"), None),
            P("wide", "narrow", None, None, "tp"),
            P("wide", "narrow", None, "tp"),
            P("wide", "narrow", None, "tp"),
            P("wide", "narrow", "tp", None),
        ),
        out_specs=(P(("wide", "narrow"), "tp"), P(("wide", "narrow"), None)),
        check_vma=False,
    )
```

```python
import jax
import jax.numpy as jnp
from jax import lax
from jax.experimental import pallas as pl
from jax.experimental.pallas import tpu as pltpu
from jax.sharding import PartitionSpec as P

LIMIT = 4
HALVES = 2
BLOCK = 8
TILE = 128


def nn(left, right):
    return lax.dot_general(
        left, right, (((1,), (0,)), ((), ())), preferred_element_type=jnp.float32
    )


def nt(left, right):
    return lax.dot_general(
        left, right, (((1,), (1,)), ((), ())), preferred_element_type=jnp.float32
    )


def iota(shape, axis):
    return lax.broadcasted_iota(jnp.int32, shape, axis)


def bits(mask):
    return jnp.where(mask, 1.0, 0.0).astype(jnp.bfloat16)


def call(kernel, outs, args, flops=0, size=1 << 20, spaces=None, out_spaces=None, scratch=(), vmem=16):
    spaces = spaces or [pltpu.VMEM] * len(args)
    return pl.pallas_call(
        kernel,
        out_shape=outs,
        in_specs=[pl.BlockSpec(memory_space=space) for space in spaces],
        out_specs=[pl.BlockSpec(memory_space=space) for space in out_spaces]
        if out_spaces
        else jax.tree.map(lambda _: pl.BlockSpec(memory_space=pltpu.VMEM), outs),
        scratch_shapes=list(scratch),
        compiler_params=pltpu.CompilerParams(vmem_limit_bytes=vmem << 20),
        cost_estimate=pl.CostEstimate(flops=flops, bytes_accessed=size, transcendentals=0),
    )(*args)


def shape(*dims, dtype=jnp.bfloat16):
    return jax.ShapeDtypeStruct(dims, dtype)


def pack_rest_kernel(gate_ref, up_ref, preact_ref, after_ref, *out_refs):
    count = len(out_refs)
    width = gate_ref.shape[0] // count
    me = lax.axis_index("tp")
    for step, out_ref in enumerate(out_refs):
        to = lax.rem(me + step, count)
        rows = pl.ds(pl.multiple_of(to * width, TILE), width)
        out_ref[0:width, :] = gate_ref[rows, :]
        out_ref[width : 2 * width, :] = up_ref[rows, :]
        out_ref[2 * width :, :] = preact_ref[...]


def join_kernel(*refs):
    out_ref = refs[-1]
    hidden = refs[0].shape[0]
    for at, block_ref in enumerate(refs[:-1]):
        out_ref[at * hidden : (at + 1) * hidden, :] = block_ref[...]


def spread(group_cap, rows):
    r, c = iota((rows, rows), 0), iota((rows, rows), 1)
    return bits((r // BLOCK == c // BLOCK) & (r % BLOCK == group_cap))


def collect(group_cap, rows):
    r, c = iota((rows, rows), 0), iota((rows, rows), 1)
    return bits(
        (r // BLOCK == c // BLOCK) & (c % BLOCK == group_cap) & (r % BLOCK < group_cap)
    )


def own_span(rows, width):
    r, c = iota((rows, rows), 0), iota((rows, rows), 1)
    return c // width == r % BLOCK


def first_kernel(group_cap, width, count, ids_hbm, gates_hbm, rows_hbm, down_hbm, *refs):
    send_ref, place_ref = refs[:2]
    down_refs = refs[2 : 2 + count]
    ids_ref, gates_ref, rows_ref, sems = refs[2 + count :]
    columns = send_ref.shape[1]
    me = lax.axis_index("tp")

    def columns_of(index):
        return pl.ds(pl.multiple_of(index * columns, TILE), columns)

    loads = [
        pltpu.make_async_copy(ids_hbm, ids_ref, sems.at[0]),
        pltpu.make_async_copy(gates_hbm, gates_ref, sems.at[1]),
        pltpu.make_async_copy(rows_hbm.at[:, columns_of(me)], rows_ref, sems.at[2]),
    ]
    packs = [
        pltpu.make_async_copy(
            down_hbm.at[:, columns_of(lax.rem(me + step, count))], down_ref, sems.at[3 + step]
        )
        for step, down_ref in enumerate(down_refs)
    ]
    for copy in loads + packs:
        copy.start()
    for copy in loads:
        copy.wait()
    top, tokens = ids_ref.shape
    rows = send_ref.shape[0]
    groups = rows // BLOCK
    ids = ids_ref[...]
    gates = gates_ref[...].astype(jnp.float32)
    member = jnp.zeros((groups, tokens), jnp.float32)
    table = jnp.zeros((groups * width, tokens), jnp.float32)
    for k in range(top):
        one = ids[k : k + 1, :]
        member = jnp.where(one // width == iota((groups, tokens), 0), 1.0, member)
        table = jnp.where(one == iota((groups * width, tokens), 0), gates[k : k + 1, :], table)
    earlier = bits(iota((tokens, tokens), 0) < iota((tokens, tokens), 1))
    rank = nn(member.astype(jnp.bfloat16), earlier)
    rank = jnp.where((member > 0) & (rank < group_cap), rank, 100.0)
    grow = bits(iota((rows, groups), 0) // BLOCK == iota((rows, groups), 1))
    place = nn(grow, rank.astype(jnp.bfloat16)) == (
        iota((rows, tokens), 0) % BLOCK
    ).astype(jnp.float32)
    place = bits(place)
    place_ref[...] = place
    send_ref[...] = nn(place, rows_ref[...]).astype(jnp.bfloat16)
    r, c = iota((rows, groups * width), 0), iota((rows, groups * width), 1)
    paired = nt(place, table.astype(jnp.bfloat16))
    paired = jnp.where(r // BLOCK == c // width, paired, 0.0).astype(jnp.bfloat16)
    a, b = iota((groups * width, rows), 0), iota((groups * width, rows), 1)
    repeated = nn(paired, bits(a % width == b % width))
    repeated = jnp.where(own_span(rows, width), repeated, 0.0).astype(jnp.bfloat16)
    notes = nn(spread(group_cap, rows), repeated)
    first = send_ref[:, 0:rows].astype(jnp.float32)
    send_ref[:, 0:rows] = (first + notes).astype(jnp.bfloat16)
    for copy in packs:
        copy.wait()


def second_kernel(group_cap, width, lane_cap, got_ref, *refs):
    out_ref, gated_ref = refs[-2:]
    rows = got_ref.shape[0]
    got = got_ref[...]
    notes = nn(collect(group_cap, rows), got[:, 0:rows])
    notes = jnp.where(own_span(rows, width), notes, 0.0).astype(jnp.bfloat16)
    slots = width * lane_cap
    a, b = iota((rows, slots), 0), iota((rows, slots), 1)
    gate = nn(notes, bits((a % width == b // lane_cap) & (a < group_cap * width)))
    hit = gate != 0.0
    rank = nn(bits(iota((rows, rows), 1) < iota((rows, rows), 0)), bits(hit))
    place = hit & (rank == (b % lane_cap).astype(jnp.float32))
    gated_ref[...] = jnp.where(place, gate, 0.0).astype(jnp.bfloat16)
    turned = jnp.transpose(jnp.where(place, 1.0, 0.0)).astype(jnp.bfloat16)
    moved = nn(turned, got).astype(jnp.bfloat16)
    for half in range(HALVES):
        out_ref[half] = moved


def partial_kernel(rows_ref, down_ref, out_ref):
    out_ref[...] = nt(rows_ref[...], down_ref[...]).astype(jnp.bfloat16)


def cycle_sum(terms):
    count = len(terms)
    while count > 1:
        count //= 2
        terms = [terms[i] + terms[i + count] for i in range(count)]
    return terms[0]


def expert_kernel(count, *refs):
    parts, blocks, out_ref = refs[:count], refs[count : 2 * count], refs[-1]
    slots = out_ref.shape[0]
    columns = out_ref.shape[1] - TILE
    hidden = parts[0].shape[1] // count
    grads, weights, scores = [], [], []
    for at in range(count):
        pieces = []
        for step in range(count):
            source = (at - step) % count
            pieces.append(
                parts[step][:, source * hidden : (source + 1) * hidden].astype(jnp.float32)
            )
        back = cycle_sum(pieces)
        gate_pre = blocks[at][2 * columns : 2 * columns + slots, :].astype(jnp.float32)
        up_pre = blocks[at][2 * columns + slots :, :].astype(jnp.float32)
        sigmoid_value = jax.nn.sigmoid(gate_pre)
        swish_value = gate_pre * sigmoid_value
        slope = sigmoid_value * (1.0 + gate_pre * (1.0 - sigmoid_value))
        up_part = swish_value * back
        scores.append(up_part * up_pre)
        grads.append((back * up_pre * slope).astype(jnp.bfloat16))
        grads.append(up_part.astype(jnp.bfloat16))
        weights.append(blocks[at][0:columns, :])
        weights.append(blocks[at][columns : 2 * columns, :])
    total = nt(jnp.concatenate(grads, axis=1), jnp.concatenate(weights, axis=1))
    out_ref[:, 0:columns] = total.astype(jnp.bfloat16)
    score = jnp.sum(cycle_sum(scores), axis=1, keepdims=True)
    out_ref[:, columns:] = jnp.broadcast_to(score, (slots, TILE)).astype(jnp.bfloat16)


def rows_kernel(group_cap, width, lane_cap, gated_ref, back_ref, out_ref):
    rows, columns = out_ref.shape
    gated = gated_ref[...]
    both = jnp.concatenate([gated, gated], axis=1)
    out_ref[...] = nn(both, back_ref[:, 0:columns]).astype(jnp.bfloat16)
    place = bits(both != 0)
    slots = both.shape[1]
    a, b = iota((slots, TILE), 0), iota((slots, TILE), 1)
    score = back_ref[:, columns:].astype(jnp.float32)
    score = jnp.where((a // lane_cap) % width == b % width, score, 0.0).astype(jnp.bfloat16)
    score = nn(place, score)
    score = jnp.where(own_span(rows, width), score, 0.0).astype(jnp.bfloat16)
    notes = nn(spread(group_cap, rows), score)
    first = out_ref[:, 0:rows].astype(jnp.float32)
    out_ref[:, 0:rows] = (first + notes).astype(jnp.bfloat16)


def last_kernel(group_cap, width, ids_ref, place_ref, home_ref, tokens_ref, gates_ref):
    top, tokens = ids_ref.shape
    rows = home_ref.shape[0]
    ids = ids_ref[...]
    home = home_ref[...]
    place = jnp.transpose(place_ref[...].astype(jnp.float32)).astype(jnp.bfloat16)
    tokens_ref[...] = nn(place, home).astype(jnp.bfloat16)
    notes = nn(collect(group_cap, rows), home[:, 0:rows])
    notes = jnp.where(own_span(rows, width), notes, 0.0).astype(jnp.bfloat16)
    a, b = iota((rows, rows), 0), iota((rows, rows), 1)
    wide = nn(notes, bits((a % width == b % width) & (a < group_cap * width)))
    wide = jnp.where(a // BLOCK == b // width, wide, 0.0).astype(jnp.bfloat16)
    score = jnp.transpose(nn(place, wide))
    at = iota((rows, tokens), 0)
    for k in range(top):
        gates_ref[k : k + 1, :] = jnp.sum(
            jnp.where(ids[k : k + 1, :] == at, score, 0.0), axis=0, keepdims=True
        )


def exchange(values, axis):
    return lax.all_to_all(values, axis, split_axis=0, concat_axis=0, tiled=True)


def shift(values, step, count):
    return lax.ppermute(
        values, "tp", [(source, (source + step) % count) for source in range(count)]
    )


def shift_all(values):
    count = len(values)
    order = sorted(range(1, count), key=lambda step: min(step, count - step))
    moved = {step: shift(values[step], step, count) for step in order}
    return [values[0]] + [moved[step] for step in range(1, count)]


def per_device(d_out, expert_ids, gate_values, stored_preacts, w_gate, w_up, w_down):
    wide_count = lax.axis_size("wide")
    lane_count = lax.axis_size("narrow")
    split_count = lax.axis_size("tp")
    group_width = lane_count // HALVES
    token_count, model_width = d_out.shape
    slot_count = stored_preacts.shape[2]
    hidden_width = stored_preacts.shape[4]
    lane_cap = slot_count // lane_count
    group_cap = min(token_count, max(1, 3 * token_count * LIMIT // (2 * wide_count)))
    columns = model_width // split_count
    rows = wide_count * BLOCK
    lanes = group_width * lane_cap
    ids = expert_ids.T

    send, place, *down_packed = call(
        lambda *refs: first_kernel(group_cap, group_width, split_count, *refs),
        [shape(rows, columns), shape(rows, token_count)]
        + [shape(hidden_width, columns)] * split_count,
        (ids, gate_values.T, d_out, w_down[0, 0]),
        spaces=[pltpu.HBM] * 4,
        out_spaces=[pltpu.VMEM] * 2 + [pltpu.HBM] * split_count,
        vmem=60,
        scratch=[
            pltpu.VMEM(ids.shape, ids.dtype),
            pltpu.VMEM(ids.shape, gate_values.dtype),
            pltpu.VMEM((token_count, columns), d_out.dtype),
            pltpu.SemaphoreType.DMA((3 + split_count,)),
        ],
    )
    downs = shift_all(down_packed)
    down_cols = call(
        join_kernel,
        shape(split_count * hidden_width, columns),
        downs,
        size=1 << 20,
        flops=20 * 10**9,
    )

    got = exchange(send.reshape(wide_count, BLOCK, columns), "wide").reshape(rows, columns)
    forward, gated = call(
        lambda *refs: second_kernel(group_cap, group_width, lane_cap, *refs),
        [shape(HALVES, lanes, columns), shape(rows, lanes)],
        (got,),
    )
    rest_packed = call(
        pack_rest_kernel,
        [shape(2 * columns + 2 * slot_count, hidden_width)] * split_count,
        (
            w_gate[0, 0],
            w_up[0, 0],
            stored_preacts[0, 0].transpose(1, 0, 2).reshape(2 * slot_count, hidden_width),
            gated,
        ),
        size=4 << 20,
        spaces=[pltpu.VMEM] * 3 + [pl.ANY],
    )
    blocks = shift_all(rest_packed)
    slot_rows = exchange(forward.reshape(lane_count, lane_cap, columns), "narrow").reshape(
        slot_count, columns
    )
    partial = call(
        partial_kernel,
        shape(slot_count, split_count * hidden_width),
        (slot_rows, down_cols),
    )
    parts = shift_all([partial] * split_count)
    terms = call(
        lambda *refs: expert_kernel(split_count, *refs),
        shape(slot_count, columns + TILE),
        (*parts, *blocks),
        vmem=24,
    )
    back = exchange(terms.reshape(lane_count, lane_cap, columns + TILE), "narrow").reshape(
        slot_count, columns + TILE
    )
    row_input = call(
        lambda *refs: rows_kernel(group_cap, group_width, lane_cap, *refs),
        shape(rows, columns),
        (gated, back),
    )
    home = exchange(row_input.reshape(wide_count, BLOCK, columns), "wide").reshape(rows, columns)
    d_tokens, d_gates = call(
        lambda *refs: last_kernel(group_cap, group_width, *refs),
        [
            shape(token_count, columns),
            shape(expert_ids.shape[1], token_count, dtype=jnp.float32),
        ],
        (ids, place, home),
    )
    return (d_tokens, d_gates.T)


def solution(mesh):
    return jax.shard_map(
        per_device,
        mesh=mesh,
        in_specs=(
            P(("wide", "narrow"), None),
            P(("wide", "narrow"), None),
            P(("wide", "narrow"), None),
            P("wide", "narrow", None, None, "tp"),
            P("wide", "narrow", None, "tp"),
            P("wide", "narrow", None, "tp"),
            P("wide", "narrow", "tp", None),
        ),
        out_specs=(P(("wide", "narrow"), "tp"), P(("wide", "narrow"), None)),
        check_vma=False,
    )
```

```python
import jax
import jax.numpy as jnp
from jax import lax
from jax.experimental import pallas as pl
from jax.experimental.pallas import tpu as pltpu
from jax.sharding import PartitionSpec as P

LIMIT = 4
HALVES = 2
BLOCK = 8
TILE = 128


def nn(left, right):
    return lax.dot_general(
        left, right, (((1,), (0,)), ((), ())), preferred_element_type=jnp.float32
    )


def nt(left, right):
    return lax.dot_general(
        left, right, (((1,), (1,)), ((), ())), preferred_element_type=jnp.float32
    )


def iota(shape, axis):
    return lax.broadcasted_iota(jnp.int32, shape, axis)


def bits(mask):
    return jnp.where(mask, 1.0, 0.0).astype(jnp.bfloat16)


def call(kernel, outs, args, flops=0, size=1 << 20, spaces=None, out_spaces=None, scratch=(), vmem=16):
    spaces = spaces or [pltpu.VMEM] * len(args)
    return pl.pallas_call(
        kernel,
        out_shape=outs,
        in_specs=[pl.BlockSpec(memory_space=space) for space in spaces],
        out_specs=[pl.BlockSpec(memory_space=space) for space in out_spaces]
        if out_spaces
        else jax.tree.map(lambda _: pl.BlockSpec(memory_space=pltpu.VMEM), outs),
        scratch_shapes=list(scratch),
        compiler_params=pltpu.CompilerParams(vmem_limit_bytes=vmem << 20),
        cost_estimate=pl.CostEstimate(flops=flops, bytes_accessed=size, transcendentals=0),
    )(*args)


def shape(*dims, dtype=jnp.bfloat16):
    return jax.ShapeDtypeStruct(dims, dtype)


def pack_rest_kernel(gate_ref, up_ref, preact_ref, after_ref, *out_refs):
    count = len(out_refs)
    width = gate_ref.shape[0] // count
    me = lax.axis_index("tp")
    for step, out_ref in enumerate(out_refs):
        to = lax.rem(me + step, count)
        rows = pl.ds(pl.multiple_of(to * width, TILE), width)
        out_ref[0:width, :] = gate_ref[rows, :]
        out_ref[width : 2 * width, :] = up_ref[rows, :]
        out_ref[2 * width :, :] = preact_ref[...]


def join_kernel(*refs):
    out_ref = refs[-1]
    hidden = refs[0].shape[0]
    for at, block_ref in enumerate(refs[:-1]):
        out_ref[at * hidden : (at + 1) * hidden, :] = block_ref[...]


def spread(group_cap, rows):
    r, c = iota((rows, rows), 0), iota((rows, rows), 1)
    return bits((r // BLOCK == c // BLOCK) & (r % BLOCK == group_cap))


def collect(group_cap, rows):
    r, c = iota((rows, rows), 0), iota((rows, rows), 1)
    return bits(
        (r // BLOCK == c // BLOCK) & (c % BLOCK == group_cap) & (r % BLOCK < group_cap)
    )


def own_span(rows, width):
    r, c = iota((rows, rows), 0), iota((rows, rows), 1)
    return c // width == r % BLOCK


def first_kernel(group_cap, width, count, ids_hbm, gates_hbm, rows_hbm, down_hbm, *refs):
    send_ref, place_ref = refs[:2]
    down_refs = refs[2 : 2 + count]
    ids_ref, gates_ref, rows_ref, sems = refs[2 + count :]
    columns = send_ref.shape[1]
    me = lax.axis_index("tp")

    def columns_of(index):
        return pl.ds(pl.multiple_of(index * columns, TILE), columns)

    loads = [
        pltpu.make_async_copy(ids_hbm, ids_ref, sems.at[0]),
        pltpu.make_async_copy(gates_hbm, gates_ref, sems.at[1]),
        pltpu.make_async_copy(rows_hbm.at[:, columns_of(me)], rows_ref, sems.at[2]),
    ]
    packs = [
        pltpu.make_async_copy(
            down_hbm.at[:, columns_of(lax.rem(me + step, count))], down_ref, sems.at[3 + step]
        )
        for step, down_ref in enumerate(down_refs)
    ]
    for copy in loads + packs:
        copy.start()
    for copy in loads:
        copy.wait()
    top, tokens = ids_ref.shape
    rows = send_ref.shape[0]
    groups = rows // BLOCK
    ids = ids_ref[...]
    gates = gates_ref[...].astype(jnp.float32)
    member = jnp.zeros((groups, tokens), jnp.float32)
    table = jnp.zeros((groups * width, tokens), jnp.float32)
    for k in range(top):
        one = ids[k : k + 1, :]
        member = jnp.where(one // width == iota((groups, tokens), 0), 1.0, member)
        table = jnp.where(one == iota((groups * width, tokens), 0), gates[k : k + 1, :], table)
    earlier = bits(iota((tokens, tokens), 0) < iota((tokens, tokens), 1))
    rank = nn(member.astype(jnp.bfloat16), earlier)
    rank = jnp.where((member > 0) & (rank < group_cap), rank, 100.0)
    grow = bits(iota((rows, groups), 0) // BLOCK == iota((rows, groups), 1))
    place = nn(grow, rank.astype(jnp.bfloat16)) == (
        iota((rows, tokens), 0) % BLOCK
    ).astype(jnp.float32)
    place = bits(place)
    place_ref[...] = place
    send_ref[...] = nn(place, rows_ref[...]).astype(jnp.bfloat16)
    r, c = iota((rows, groups * width), 0), iota((rows, groups * width), 1)
    paired = nt(place, table.astype(jnp.bfloat16))
    paired = jnp.where(r // BLOCK == c // width, paired, 0.0).astype(jnp.bfloat16)
    a, b = iota((groups * width, rows), 0), iota((groups * width, rows), 1)
    repeated = nn(paired, bits(a % width == b % width))
    repeated = jnp.where(own_span(rows, width), repeated, 0.0).astype(jnp.bfloat16)
    notes = nn(spread(group_cap, rows), repeated)
    first = send_ref[:, 0:rows].astype(jnp.float32)
    send_ref[:, 0:rows] = (first + notes).astype(jnp.bfloat16)
    for copy in packs:
        copy.wait()


def second_kernel(group_cap, width, lane_cap, got_ref, *refs):
    out_ref, gated_ref = refs[-2:]
    rows = got_ref.shape[0]
    got = got_ref[...]
    notes = nn(collect(group_cap, rows), got[:, 0:rows])
    notes = jnp.where(own_span(rows, width), notes, 0.0).astype(jnp.bfloat16)
    slots = width * lane_cap
    a, b = iota((rows, slots), 0), iota((rows, slots), 1)
    gate = nn(notes, bits((a % width == b // lane_cap) & (a < group_cap * width)))
    hit = gate != 0.0
    rank = nn(bits(iota((rows, rows), 1) < iota((rows, rows), 0)), bits(hit))
    place = hit & (rank == (b % lane_cap).astype(jnp.float32))
    gated_ref[...] = jnp.where(place, gate, 0.0).astype(jnp.bfloat16)
    turned = jnp.transpose(jnp.where(place, 1.0, 0.0)).astype(jnp.bfloat16)
    moved = nn(turned, got).astype(jnp.bfloat16)
    for half in range(HALVES):
        out_ref[half] = moved


def partial_kernel(rows_ref, down_ref, out_ref):
    out_ref[...] = nt(rows_ref[...], down_ref[...]).astype(jnp.bfloat16)


def cycle_sum(terms):
    count = len(terms)
    while count > 1:
        count //= 2
        terms = [terms[i] + terms[i + count] for i in range(count)]
    return terms[0]


def expert_kernel(count, *refs):
    parts, blocks, out_ref = refs[:count], refs[count : 2 * count], refs[-1]
    slots = out_ref.shape[0]
    columns = out_ref.shape[1] - TILE
    hidden = parts[0].shape[1] // count
    grads, weights, scores = [], [], []
    for at in range(count):
        pieces = []
        for step in range(count):
            source = (at - step) % count
            pieces.append(
                parts[step][:, source * hidden : (source + 1) * hidden].astype(jnp.float32)
            )
        back = cycle_sum(pieces)
        gate_pre = blocks[at][2 * columns : 2 * columns + slots, :].astype(jnp.float32)
        up_pre = blocks[at][2 * columns + slots :, :].astype(jnp.float32)
        sigmoid_value = jax.nn.sigmoid(gate_pre)
        swish_value = gate_pre * sigmoid_value
        slope = sigmoid_value * (1.0 + gate_pre * (1.0 - sigmoid_value))
        up_part = swish_value * back
        scores.append(up_part * up_pre)
        grads.append((back * up_pre * slope).astype(jnp.bfloat16))
        grads.append(up_part.astype(jnp.bfloat16))
        weights.append(blocks[at][0:columns, :])
        weights.append(blocks[at][columns : 2 * columns, :])
    total = nt(jnp.concatenate(grads, axis=1), jnp.concatenate(weights, axis=1))
    out_ref[:, 0:columns] = total.astype(jnp.bfloat16)
    score = jnp.sum(cycle_sum(scores), axis=1, keepdims=True)
    out_ref[:, columns:] = jnp.broadcast_to(score, (slots, TILE)).astype(jnp.bfloat16)


def rows_kernel(group_cap, width, lane_cap, gated_ref, back_ref, out_ref):
    rows, columns = out_ref.shape
    gated = gated_ref[...]
    both = jnp.concatenate([gated, gated], axis=1)
    out_ref[...] = nn(both, back_ref[:, 0:columns]).astype(jnp.bfloat16)
    place = bits(both != 0)
    slots = both.shape[1]
    a, b = iota((slots, TILE), 0), iota((slots, TILE), 1)
    score = back_ref[:, columns:].astype(jnp.float32)
    score = jnp.where((a // lane_cap) % width == b % width, score, 0.0).astype(jnp.bfloat16)
    score = nn(place, score)
    score = jnp.where(own_span(rows, width), score, 0.0).astype(jnp.bfloat16)
    notes = nn(spread(group_cap, rows), score)
    first = out_ref[:, 0:rows].astype(jnp.float32)
    out_ref[:, 0:rows] = (first + notes).astype(jnp.bfloat16)


def last_kernel(group_cap, width, ids_ref, place_ref, home_ref, tokens_ref, gates_ref):
    top, tokens = ids_ref.shape
    rows = home_ref.shape[0]
    ids = ids_ref[...]
    home = home_ref[...]
    place = jnp.transpose(place_ref[...].astype(jnp.float32)).astype(jnp.bfloat16)
    tokens_ref[...] = nn(place, home).astype(jnp.bfloat16)
    notes = nn(collect(group_cap, rows), home[:, 0:rows])
    notes = jnp.where(own_span(rows, width), notes, 0.0).astype(jnp.bfloat16)
    a, b = iota((rows, rows), 0), iota((rows, rows), 1)
    wide = nn(notes, bits((a % width == b % width) & (a < group_cap * width)))
    wide = jnp.where(a // BLOCK == b // width, wide, 0.0).astype(jnp.bfloat16)
    score = jnp.transpose(nn(place, wide))
    at = iota((rows, tokens), 0)
    for k in range(top):
        gates_ref[k : k + 1, :] = jnp.sum(
            jnp.where(ids[k : k + 1, :] == at, score, 0.0), axis=0, keepdims=True
        )


def exchange(values, axis):
    return lax.all_to_all(values, axis, split_axis=0, concat_axis=0, tiled=True)


def shift(values, step, count):
    return lax.ppermute(
        values, "tp", [(source, (source + step) % count) for source in range(count)]
    )


def shift_all(values):
    count = len(values)
    order = sorted(range(1, count), key=lambda step: min(step, count - step))
    moved = {step: shift(values[step], step, count) for step in order}
    return [values[0]] + [moved[step] for step in range(1, count)]


def per_device(d_out, expert_ids, gate_values, stored_preacts, w_gate, w_up, w_down):
    wide_count = lax.axis_size("wide")
    lane_count = lax.axis_size("narrow")
    split_count = lax.axis_size("tp")
    group_width = lane_count // HALVES
    token_count, model_width = d_out.shape
    slot_count = stored_preacts.shape[2]
    hidden_width = stored_preacts.shape[4]
    lane_cap = slot_count // lane_count
    group_cap = min(token_count, max(1, 3 * token_count * LIMIT // (2 * wide_count)))
    columns = model_width // split_count
    rows = wide_count * BLOCK
    lanes = group_width * lane_cap
    ids = expert_ids.T

    send, place, *down_packed = call(
        lambda *refs: first_kernel(group_cap, group_width, split_count, *refs),
        [shape(rows, columns), shape(rows, token_count)]
        + [shape(hidden_width, columns)] * split_count,
        (ids, gate_values.T, d_out, w_down[0, 0]),
        spaces=[pltpu.HBM] * 4,
        out_spaces=[pltpu.VMEM] * (2 + split_count),
        vmem=60,
        scratch=[
            pltpu.VMEM(ids.shape, ids.dtype),
            pltpu.VMEM(ids.shape, gate_values.dtype),
            pltpu.VMEM((token_count, columns), d_out.dtype),
            pltpu.SemaphoreType.DMA((3 + split_count,)),
        ],
    )
    downs = shift_all(down_packed)
    down_cols = call(
        join_kernel,
        shape(split_count * hidden_width, columns),
        downs,
        size=1 << 20,
        flops=20 * 10**9,
    )

    got = exchange(send.reshape(wide_count, BLOCK, columns), "wide").reshape(rows, columns)
    forward, gated = call(
        lambda *refs: second_kernel(group_cap, group_width, lane_cap, *refs),
        [shape(HALVES, lanes, columns), shape(rows, lanes)],
        (got,),
    )
    rest_packed = call(
        pack_rest_kernel,
        [shape(2 * columns + 2 * slot_count, hidden_width)] * split_count,
        (
            w_gate[0, 0],
            w_up[0, 0],
            stored_preacts[0, 0].transpose(1, 0, 2).reshape(2 * slot_count, hidden_width),
            gated,
        ),
        size=4 << 20,
        spaces=[pltpu.VMEM] * 3 + [pl.ANY],
    )
    blocks = shift_all(rest_packed)
    slot_rows = exchange(forward.reshape(lane_count, lane_cap, columns), "narrow").reshape(
        slot_count, columns
    )
    partial = call(
        partial_kernel,
        shape(slot_count, split_count * hidden_width),
        (slot_rows, down_cols),
    )
    parts = shift_all([partial] * split_count)
    terms = call(
        lambda *refs: expert_kernel(split_count, *refs),
        shape(slot_count, columns + TILE),
        (*parts, *blocks),
        vmem=24,
    )
    back = exchange(terms.reshape(lane_count, lane_cap, columns + TILE), "narrow").reshape(
        slot_count, columns + TILE
    )
    row_input = call(
        lambda *refs: rows_kernel(group_cap, group_width, lane_cap, *refs),
        shape(rows, columns),
        (gated, back),
    )
    home = exchange(row_input.reshape(wide_count, BLOCK, columns), "wide").reshape(rows, columns)
    d_tokens, d_gates = call(
        lambda *refs: last_kernel(group_cap, group_width, *refs),
        [
            shape(token_count, columns),
            shape(expert_ids.shape[1], token_count, dtype=jnp.float32),
        ],
        (ids, place, home),
    )
    return (d_tokens, d_gates.T)


def solution(mesh):
    return jax.shard_map(
        per_device,
        mesh=mesh,
        in_specs=(
            P(("wide", "narrow"), None),
            P(("wide", "narrow"), None),
            P(("wide", "narrow"), None),
            P("wide", "narrow", None, None, "tp"),
            P("wide", "narrow", None, "tp"),
            P("wide", "narrow", None, "tp"),
            P("wide", "narrow", "tp", None),
        ),
        out_specs=(P(("wide", "narrow"), "tp"), P(("wide", "narrow"), None)),
        check_vma=False,
    )
```

```python
import jax
import jax.numpy as jnp
from jax import lax
from jax.experimental import pallas as pl
from jax.experimental.pallas import tpu as pltpu
from jax.sharding import PartitionSpec as P

LIMIT = 4
HALVES = 2
BLOCK = 8
TILE = 128


def nn(left, right):
    return lax.dot_general(
        left, right, (((1,), (0,)), ((), ())), preferred_element_type=jnp.float32
    )


def nt(left, right):
    return lax.dot_general(
        left, right, (((1,), (1,)), ((), ())), preferred_element_type=jnp.float32
    )


def iota(shape, axis):
    return lax.broadcasted_iota(jnp.int32, shape, axis)


def bits(mask):
    return jnp.where(mask, 1.0, 0.0).astype(jnp.bfloat16)


def call(kernel, outs, args, flops=0, size=1 << 20, spaces=None, out_spaces=None, scratch=(), vmem=16):
    spaces = spaces or [pltpu.VMEM] * len(args)
    return pl.pallas_call(
        kernel,
        out_shape=outs,
        in_specs=[pl.BlockSpec(memory_space=space) for space in spaces],
        out_specs=[pl.BlockSpec(memory_space=space) for space in out_spaces]
        if out_spaces
        else jax.tree.map(lambda _: pl.BlockSpec(memory_space=pltpu.VMEM), outs),
        scratch_shapes=list(scratch),
        compiler_params=pltpu.CompilerParams(vmem_limit_bytes=vmem << 20),
        cost_estimate=pl.CostEstimate(flops=flops, bytes_accessed=size, transcendentals=0),
    )(*args)


def shape(*dims, dtype=jnp.bfloat16):
    return jax.ShapeDtypeStruct(dims, dtype)


def pack_rest_kernel(gate_ref, up_ref, preact_ref, after_ref, *out_refs):
    count = len(out_refs)
    width = gate_ref.shape[0] // count
    me = lax.axis_index("tp")
    for step, out_ref in enumerate(out_refs):
        to = lax.rem(me + step, count)
        rows = pl.ds(pl.multiple_of(to * width, TILE), width)
        out_ref[0:width, :] = gate_ref[rows, :]
        out_ref[width : 2 * width, :] = up_ref[rows, :]
        out_ref[2 * width :, :] = preact_ref[...]


def join_kernel(*refs):
    out_ref = refs[-1]
    hidden = refs[0].shape[0]
    for at, block_ref in enumerate(refs[:-1]):
        out_ref[at * hidden : (at + 1) * hidden, :] = block_ref[...]


def spread(group_cap, rows):
    r, c = iota((rows, rows), 0), iota((rows, rows), 1)
    return bits((r // BLOCK == c // BLOCK) & (r % BLOCK == group_cap))


def collect(group_cap, rows):
    r, c = iota((rows, rows), 0), iota((rows, rows), 1)
    return bits(
        (r // BLOCK == c // BLOCK) & (c % BLOCK == group_cap) & (r % BLOCK < group_cap)
    )


def own_span(rows, width):
    r, c = iota((rows, rows), 0), iota((rows, rows), 1)
    return c // width == r % BLOCK


def first_kernel(group_cap, width, count, ids_hbm, gates_hbm, rows_hbm, down_hbm, *refs):
    send_ref, place_ref = refs[:2]
    down_refs = refs[2 : 2 + count]
    ids_ref, gates_ref, rows_ref, sems = refs[2 + count :]
    columns = send_ref.shape[1]
    me = lax.axis_index("tp")

    def columns_of(index):
        return pl.ds(pl.multiple_of(index * columns, TILE), columns)

    loads = [
        pltpu.make_async_copy(ids_hbm, ids_ref, sems.at[0]),
        pltpu.make_async_copy(gates_hbm, gates_ref, sems.at[1]),
        pltpu.make_async_copy(rows_hbm.at[:, columns_of(me)], rows_ref, sems.at[2]),
    ]
    packs = [
        pltpu.make_async_copy(
            down_hbm.at[:, columns_of(lax.rem(me + step, count))], down_ref, sems.at[3 + step]
        )
        for step, down_ref in enumerate(down_refs)
    ]
    for copy in loads + packs:
        copy.start()
    for copy in loads:
        copy.wait()
    top, tokens = ids_ref.shape
    rows = send_ref.shape[0]
    groups = rows // BLOCK
    ids = ids_ref[...]
    gates = gates_ref[...].astype(jnp.float32)
    member = jnp.zeros((groups, tokens), jnp.float32)
    table = jnp.zeros((groups * width, tokens), jnp.float32)
    for k in range(top):
        one = ids[k : k + 1, :]
        member = jnp.where(one // width == iota((groups, tokens), 0), 1.0, member)
        table = jnp.where(one == iota((groups * width, tokens), 0), gates[k : k + 1, :], table)
    earlier = bits(iota((tokens, tokens), 0) < iota((tokens, tokens), 1))
    rank = nn(member.astype(jnp.bfloat16), earlier)
    rank = jnp.where((member > 0) & (rank < group_cap), rank, 100.0)
    grow = bits(iota((rows, groups), 0) // BLOCK == iota((rows, groups), 1))
    place = nn(grow, rank.astype(jnp.bfloat16)) == (
        iota((rows, tokens), 0) % BLOCK
    ).astype(jnp.float32)
    place = bits(place)
    place_ref[...] = place
    send_ref[...] = nn(place, rows_ref[...]).astype(jnp.bfloat16)
    r, c = iota((rows, groups * width), 0), iota((rows, groups * width), 1)
    paired = nt(place, table.astype(jnp.bfloat16))
    paired = jnp.where(r // BLOCK == c // width, paired, 0.0).astype(jnp.bfloat16)
    a, b = iota((groups * width, rows), 0), iota((groups * width, rows), 1)
    repeated = nn(paired, bits(a % width == b % width))
    repeated = jnp.where(own_span(rows, width), repeated, 0.0).astype(jnp.bfloat16)
    notes = nn(spread(group_cap, rows), repeated)
    first = send_ref[:, 0:rows].astype(jnp.float32)
    send_ref[:, 0:rows] = (first + notes).astype(jnp.bfloat16)
    for copy in packs:
        copy.wait()


def second_kernel(group_cap, width, lane_cap, got_ref, *refs):
    out_ref, gated_ref = refs[-2:]
    rows = got_ref.shape[0]
    got = got_ref[...]
    notes = nn(collect(group_cap, rows), got[:, 0:rows])
    notes = jnp.where(own_span(rows, width), notes, 0.0).astype(jnp.bfloat16)
    slots = width * lane_cap
    a, b = iota((rows, slots), 0), iota((rows, slots), 1)
    gate = nn(notes, bits((a % width == b // lane_cap) & (a < group_cap * width)))
    hit = gate != 0.0
    rank = nn(bits(iota((rows, rows), 1) < iota((rows, rows), 0)), bits(hit))
    place = hit & (rank == (b % lane_cap).astype(jnp.float32))
    gated_ref[...] = jnp.where(place, gate, 0.0).astype(jnp.bfloat16)
    turned = jnp.transpose(jnp.where(place, 1.0, 0.0)).astype(jnp.bfloat16)
    moved = nn(turned, got).astype(jnp.bfloat16)
    for half in range(HALVES):
        out_ref[half] = moved


def partial_kernel(rows_ref, down_ref, out_ref):
    out_ref[...] = nt(rows_ref[...], down_ref[...]).astype(jnp.bfloat16)


def cycle_sum(terms):
    count = len(terms)
    while count > 1:
        count //= 2
        terms = [terms[i] + terms[i + count] for i in range(count)]
    return terms[0]


def prepare_kernel(*refs):
    blocks, (weight_ref, swish_ref, slope_ref, hidden_ref) = refs[:-4], refs[-4:]
    columns = weight_ref.shape[0]
    slots = swish_ref.shape[0]
    for at, block_ref in enumerate(blocks):
        for part in range(2):
            first = (2 * at + part) * TILE
            weight_ref[:, first : first + TILE] = block_ref[part * columns : (part + 1) * columns, :]
        gate_pre = block_ref[2 * columns : 2 * columns + slots, :].astype(jnp.float32)
        up_pre = block_ref[2 * columns + slots :, :].astype(jnp.float32)
        sigmoid_value = jax.nn.sigmoid(gate_pre)
        swish_value = gate_pre * sigmoid_value
        lanes = slice(at * TILE, (at + 1) * TILE)
        swish_ref[:, lanes] = swish_value
        slope_ref[:, lanes] = up_pre * (sigmoid_value * (1.0 + gate_pre * (1.0 - sigmoid_value)))
        hidden_ref[:, lanes] = swish_value * up_pre


def expert_kernel(count, lane_cap, *refs):
    parts = refs[:count]
    weight_ref, swish_ref, slope_ref, hidden_ref, out_ref = refs[count:]
    slots = parts[0].shape[0]
    columns = weight_ref.shape[0]
    grads, scores = [], []
    for at in range(count):
        pieces = []
        for step in range(count):
            source = (at - step) % count
            pieces.append(
                parts[step][:, source * TILE : (source + 1) * TILE].astype(jnp.float32)
            )
        back = cycle_sum(pieces)
        lanes = slice(at * TILE, (at + 1) * TILE)
        scores.append(hidden_ref[:, lanes] * back)
        grads.append((slope_ref[:, lanes] * back).astype(jnp.bfloat16))
        grads.append((swish_ref[:, lanes] * back).astype(jnp.bfloat16))
    total = nt(jnp.concatenate(grads, axis=1), weight_ref[...]).astype(jnp.bfloat16)
    lane_count = slots // lane_cap
    pieces = [
        total[:, first : first + TILE].reshape(lane_count, lane_cap, TILE)
        for first in range(0, columns, TILE)
    ]
    score = jnp.sum(cycle_sum(scores), axis=1, keepdims=True)
    lane = lax.rem(lax.axis_index("narrow"), lane_count // HALVES)
    slot, place = iota((slots, TILE), 0), iota((slots, TILE), 1)
    score = jnp.where(place == lane * lane_cap + slot % lane_cap, score, 0.0)
    score = jnp.sum(score.reshape(lane_count, lane_cap, TILE), axis=1, keepdims=True)
    pieces.append(jnp.broadcast_to(score, (lane_count, BLOCK, TILE)).astype(jnp.bfloat16))
    out_ref[...] = jnp.concatenate(pieces, axis=1)


def rows_kernel(group_cap, width, lane_cap, gated_ref, back_ref, out_ref):
    rows, columns = out_ref.shape
    gated = gated_ref[...]
    lane_count = back_ref.shape[0]
    pieces = [
        back_ref[:, tile * lane_cap : (tile + 1) * lane_cap, :].reshape(lane_count * lane_cap, TILE)
        for tile in range(columns // TILE)
    ]
    both = jnp.concatenate([gated, gated], axis=1)
    out_ref[...] = nn(both, jnp.concatenate(pieces, axis=1)).astype(jnp.bfloat16)
    score = back_ref[...][:, columns // TILE * lane_cap :, :].astype(jnp.float32)
    score = jnp.sum(jnp.sum(score, axis=0)[0:1, :], axis=0, keepdims=True)
    score = jnp.where(gated != 0, score, 0.0).astype(jnp.bfloat16)
    a, b = iota((rows, TILE), 0), iota((rows, TILE), 1)
    score = nn(score, bits(a // lane_cap == b % width))
    score = jnp.where(own_span(rows, width), score, 0.0).astype(jnp.bfloat16)
    notes = nn(spread(group_cap, rows), score)
    first = out_ref[:, 0:rows].astype(jnp.float32)
    out_ref[:, 0:rows] = (first + notes).astype(jnp.bfloat16)


def last_kernel(group_cap, width, ids_ref, place_ref, home_ref, tokens_ref, gates_ref):
    top, tokens = ids_ref.shape
    rows = home_ref.shape[0]
    ids = ids_ref[...]
    home = home_ref[...]
    place = jnp.transpose(place_ref[...].astype(jnp.float32)).astype(jnp.bfloat16)
    tokens_ref[...] = nn(place, home).astype(jnp.bfloat16)
    notes = nn(collect(group_cap, rows), home[:, 0:rows])
    notes = jnp.where(own_span(rows, width), notes, 0.0).astype(jnp.bfloat16)
    a, b = iota((rows, rows), 0), iota((rows, rows), 1)
    wide = nn(notes, bits((a % width == b % width) & (a < group_cap * width)))
    wide = jnp.where(a // BLOCK == b // width, wide, 0.0).astype(jnp.bfloat16)
    score = jnp.transpose(nn(place, wide))
    at = iota((rows, tokens), 0)
    for k in range(top):
        gates_ref[k : k + 1, :] = jnp.sum(
            jnp.where(ids[k : k + 1, :] == at, score, 0.0), axis=0, keepdims=True
        )


def exchange(values, axis):
    return lax.all_to_all(values, axis, split_axis=0, concat_axis=0, tiled=True)


def shift(values, step, count):
    return lax.ppermute(
        values, "tp", [(source, (source + step) % count) for source in range(count)]
    )


def shift_all(values):
    count = len(values)
    order = sorted(range(1, count), key=lambda step: min(step, count - step))
    moved = {step: shift(values[step], step, count) for step in order}
    return [values[0]] + [moved[step] for step in range(1, count)]


def per_device(d_out, expert_ids, gate_values, stored_preacts, w_gate, w_up, w_down):
    wide_count = lax.axis_size("wide")
    lane_count = lax.axis_size("narrow")
    split_count = lax.axis_size("tp")
    group_width = lane_count // HALVES
    token_count, model_width = d_out.shape
    slot_count = stored_preacts.shape[2]
    hidden_width = stored_preacts.shape[4]
    lane_cap = slot_count // lane_count
    group_cap = min(token_count, max(1, 3 * token_count * LIMIT // (2 * wide_count)))
    columns = model_width // split_count
    rows = wide_count * BLOCK
    lanes = group_width * lane_cap
    ids = expert_ids.T

    send, place, *down_packed = call(
        lambda *refs: first_kernel(group_cap, group_width, split_count, *refs),
        [shape(rows, columns), shape(rows, token_count)]
        + [shape(hidden_width, columns)] * split_count,
        (ids, gate_values.T, d_out, w_down[0, 0]),
        spaces=[pltpu.HBM] * 4,
        out_spaces=[pltpu.VMEM] * (2 + split_count),
        vmem=60,
        scratch=[
            pltpu.VMEM(ids.shape, ids.dtype),
            pltpu.VMEM(ids.shape, gate_values.dtype),
            pltpu.VMEM((token_count, columns), d_out.dtype),
            pltpu.SemaphoreType.DMA((3 + split_count,)),
        ],
    )
    downs = shift_all(down_packed)
    down_cols = call(
        join_kernel,
        shape(split_count * hidden_width, columns),
        downs,
        size=1 << 20,
        flops=20 * 10**9,
    )

    got = exchange(send.reshape(wide_count, BLOCK, columns), "wide").reshape(rows, columns)
    forward, gated = call(
        lambda *refs: second_kernel(group_cap, group_width, lane_cap, *refs),
        [shape(HALVES, lanes, columns), shape(rows, lanes)],
        (got,),
    )
    rest_packed = call(
        pack_rest_kernel,
        [shape(2 * columns + 2 * slot_count, hidden_width)] * split_count,
        (
            w_gate[0, 0],
            w_up[0, 0],
            stored_preacts[0, 0].transpose(1, 0, 2).reshape(2 * slot_count, hidden_width),
            gated,
        ),
        size=4 << 20,
        spaces=[pltpu.VMEM] * 3 + [pl.ANY],
    )
    blocks = shift_all(rest_packed)
    slot_rows = exchange(forward.reshape(lane_count, lane_cap, columns), "narrow").reshape(
        slot_count, columns
    )
    partial = call(
        partial_kernel,
        shape(slot_count, split_count * hidden_width),
        (slot_rows, down_cols),
    )
    parts = shift_all([partial] * split_count)
    hidden_all = split_count * hidden_width
    prepared = call(
        prepare_kernel,
        [shape(columns, 2 * hidden_all)]
        + [shape(slot_count, hidden_all, dtype=jnp.float32)] * 3,
        blocks,
        size=8 << 20,
    )
    block_rows = columns // TILE * lane_cap + BLOCK
    terms = call(
        lambda *refs: expert_kernel(split_count, lane_cap, *refs),
        shape(lane_count, block_rows, TILE),
        (*parts, *prepared),
        vmem=24,
    )
    back = exchange(terms, "narrow")
    row_input = call(
        lambda *refs: rows_kernel(group_cap, group_width, lane_cap, *refs),
        shape(rows, columns),
        (gated, back),
    )
    home = exchange(row_input.reshape(wide_count, BLOCK, columns), "wide").reshape(rows, columns)
    d_tokens, d_gates = call(
        lambda *refs: last_kernel(group_cap, group_width, *refs),
        [
            shape(token_count, columns),
            shape(expert_ids.shape[1], token_count, dtype=jnp.float32),
        ],
        (ids, place, home),
    )
    return (d_tokens, d_gates.T)


def solution(mesh):
    return jax.shard_map(
        per_device,
        mesh=mesh,
        in_specs=(
            P(("wide", "narrow"), None),
            P(("wide", "narrow"), None),
            P(("wide", "narrow"), None),
            P("wide", "narrow", None, None, "tp"),
            P("wide", "narrow", None, "tp"),
            P("wide", "narrow", None, "tp"),
            P("wide", "narrow", "tp", None),
        ),
        out_specs=(P(("wide", "narrow"), "tp"), P(("wide", "narrow"), None)),
        check_vma=False,
    )
```

```python
import jax
import jax.numpy as jnp
from jax import lax
from jax.experimental import pallas as pl
from jax.experimental.pallas import tpu as pltpu
from jax.sharding import PartitionSpec as P

LIMIT = 4
HALVES = 2
BLOCK = 8
TILE = 128


def nn(left, right):
    return lax.dot_general(
        left, right, (((1,), (0,)), ((), ())), preferred_element_type=jnp.float32
    )


def nt(left, right):
    return lax.dot_general(
        left, right, (((1,), (1,)), ((), ())), preferred_element_type=jnp.float32
    )


def iota(shape, axis):
    return lax.broadcasted_iota(jnp.int32, shape, axis)


def bits(mask):
    return jnp.where(mask, 1.0, 0.0).astype(jnp.bfloat16)


def call(kernel, outs, args, flops=0, size=1 << 20, spaces=None, out_spaces=None, scratch=(), vmem=16):
    spaces = spaces or [pltpu.VMEM] * len(args)
    return pl.pallas_call(
        kernel,
        out_shape=outs,
        in_specs=[pl.BlockSpec(memory_space=space) for space in spaces],
        out_specs=[pl.BlockSpec(memory_space=space) for space in out_spaces]
        if out_spaces
        else jax.tree.map(lambda _: pl.BlockSpec(memory_space=pltpu.VMEM), outs),
        scratch_shapes=list(scratch),
        compiler_params=pltpu.CompilerParams(vmem_limit_bytes=vmem << 20),
        cost_estimate=pl.CostEstimate(flops=flops, bytes_accessed=size, transcendentals=0),
    )(*args)


def shape(*dims, dtype=jnp.bfloat16):
    return jax.ShapeDtypeStruct(dims, dtype)


def pack_rest_kernel(gate_ref, up_ref, after_ref, *out_refs):
    count = len(out_refs)
    width = gate_ref.shape[0] // count
    me = lax.axis_index("tp")
    for step, out_ref in enumerate(out_refs):
        to = lax.rem(me + step, count)
        rows = pl.ds(pl.multiple_of(to * width, TILE), width)
        out_ref[0:width, :] = gate_ref[rows, :]
        out_ref[width : 2 * width, :] = up_ref[rows, :]


def join_kernel(down_ref, *refs):
    block_refs, out_ref = refs[:-1], refs[-1]
    hidden, columns = down_ref.shape[0], out_ref.shape[1]
    own = lax.axis_index("tp") * columns
    out_ref[0:hidden, :] = down_ref[:, pl.ds(pl.multiple_of(own, TILE), columns)]
    for at, block_ref in enumerate(block_refs, 1):
        for tile in range(columns // TILE):
            out_ref[at * hidden : (at + 1) * hidden, tile * TILE : (tile + 1) * TILE] = (
                block_ref[tile * hidden : (tile + 1) * hidden, :]
            )


def spread(group_cap, rows):
    r, c = iota((rows, rows), 0), iota((rows, rows), 1)
    return bits((r // BLOCK == c // BLOCK) & (r % BLOCK == group_cap))


def collect(group_cap, rows):
    r, c = iota((rows, rows), 0), iota((rows, rows), 1)
    return bits(
        (r // BLOCK == c // BLOCK) & (c % BLOCK == group_cap) & (r % BLOCK < group_cap)
    )


def own_span(rows, width):
    r, c = iota((rows, rows), 0), iota((rows, rows), 1)
    return c // width == r % BLOCK


def first_kernel(
    group_cap, width, count, ids_hbm, gates_hbm, rows_hbm, down_hbm, preacts_hbm, *refs
):
    send_ref, place_ref = refs[:2]
    block_refs = refs[2 : 1 + count]
    ids_ref, gates_ref, rows_ref, sems = refs[1 + count :]
    columns = send_ref.shape[1]
    me = lax.axis_index("tp")

    def columns_of(index):
        return pl.ds(pl.multiple_of(index * columns, TILE), columns)

    loads = [
        pltpu.make_async_copy(ids_hbm, ids_ref, sems.at[0]),
        pltpu.make_async_copy(gates_hbm, gates_ref, sems.at[1]),
        pltpu.make_async_copy(rows_hbm.at[:, columns_of(me)], rows_ref, sems.at[2]),
    ]
    packs = []
    hidden = down_hbm.shape[0]
    for step, block_ref in enumerate(block_refs, 1):
        first = lax.rem(me + step, count) * columns
        for tile in range(columns // TILE):
            lanes = pl.ds(pl.multiple_of(first + tile * TILE, TILE), TILE)
            packs.append((down_hbm.at[:, lanes], block_ref.at[pl.ds(tile * hidden, hidden)]))
        tail = pl.ds(columns // TILE * hidden, preacts_hbm.shape[0])
        packs.append((preacts_hbm, block_ref.at[tail]))
    packs = [
        pltpu.make_async_copy(source, target, sems.at[3 + at])
        for at, (source, target) in enumerate(packs)
    ]
    for copy in loads + packs:
        copy.start()
    for copy in loads:
        copy.wait()
    top, tokens = ids_ref.shape
    rows = send_ref.shape[0]
    groups = rows // BLOCK
    ids = ids_ref[...]
    gates = gates_ref[...].astype(jnp.float32)
    member = jnp.zeros((groups, tokens), jnp.float32)
    table = jnp.zeros((groups * width, tokens), jnp.float32)
    for k in range(top):
        one = ids[k : k + 1, :]
        member = jnp.where(one // width == iota((groups, tokens), 0), 1.0, member)
        table = jnp.where(one == iota((groups * width, tokens), 0), gates[k : k + 1, :], table)
    earlier = bits(iota((tokens, tokens), 0) < iota((tokens, tokens), 1))
    rank = nn(member.astype(jnp.bfloat16), earlier)
    rank = jnp.where((member > 0) & (rank < group_cap), rank, 100.0)
    grow = bits(iota((rows, groups), 0) // BLOCK == iota((rows, groups), 1))
    place = nn(grow, rank.astype(jnp.bfloat16)) == (
        iota((rows, tokens), 0) % BLOCK
    ).astype(jnp.float32)
    place = bits(place)
    place_ref[...] = place
    send_ref[...] = nn(place, rows_ref[...]).astype(jnp.bfloat16)
    r, c = iota((rows, groups * width), 0), iota((rows, groups * width), 1)
    paired = nt(place, table.astype(jnp.bfloat16))
    paired = jnp.where(r // BLOCK == c // width, paired, 0.0).astype(jnp.bfloat16)
    a, b = iota((groups * width, rows), 0), iota((groups * width, rows), 1)
    repeated = nn(paired, bits(a % width == b % width))
    repeated = jnp.where(own_span(rows, width), repeated, 0.0).astype(jnp.bfloat16)
    notes = nn(spread(group_cap, rows), repeated)
    first = send_ref[:, 0:rows].astype(jnp.float32)
    send_ref[:, 0:rows] = (first + notes).astype(jnp.bfloat16)
    for copy in packs:
        copy.wait()


def second_kernel(group_cap, width, lane_cap, got_ref, *refs):
    out_ref, gated_ref = refs[-2:]
    rows = got_ref.shape[0]
    got = got_ref[...]
    notes = nn(collect(group_cap, rows), got[:, 0:rows])
    notes = jnp.where(own_span(rows, width), notes, 0.0).astype(jnp.bfloat16)
    slots = width * lane_cap
    a, b = iota((rows, slots), 0), iota((rows, slots), 1)
    gate = nn(notes, bits((a % width == b // lane_cap) & (a < group_cap * width)))
    hit = gate != 0.0
    rank = nn(bits(iota((rows, rows), 1) < iota((rows, rows), 0)), bits(hit))
    place = hit & (rank == (b % lane_cap).astype(jnp.float32))
    gated_ref[...] = jnp.where(place, gate, 0.0).astype(jnp.bfloat16)
    turned = jnp.transpose(jnp.where(place, 1.0, 0.0)).astype(jnp.bfloat16)
    moved = nn(turned, got).astype(jnp.bfloat16)
    for half in range(HALVES):
        out_ref[half] = moved


def partial_kernel(rows_ref, down_ref, out_ref):
    out_ref[...] = nt(rows_ref[...], down_ref[...]).astype(jnp.bfloat16)


def cycle_sum(terms):
    count = len(terms)
    while count > 1:
        count //= 2
        terms = [terms[i] + terms[i + count] for i in range(count)]
    return terms[0]


def prepare_kernel(count, preacts_ref, *refs):
    blocks, early = refs[:count], refs[count : 2 * count - 1]
    weight_ref, swish_ref, slope_ref, hidden_ref = refs[2 * count - 1 :]
    columns = weight_ref.shape[0]
    slots = swish_ref.shape[0]
    for at, block_ref in enumerate(blocks):
        for part in range(2):
            first = (2 * at + part) * TILE
            weight_ref[:, first : first + TILE] = block_ref[part * columns : (part + 1) * columns, :]
    tail = early[0].shape[0] - 2 * slots
    raw = jnp.concatenate(
        [preacts_ref[...]] + [block_ref[tail:, :] for block_ref in early], axis=1
    )
    slot, row = iota((slots, 2 * slots), 0), iota((slots, 2 * slots), 1)
    gate_pre = nn(bits(row == 2 * slot), raw)
    up_pre = nn(bits(row == 2 * slot + 1), raw)
    sigmoid_value = jax.nn.sigmoid(gate_pre)
    swish_value = gate_pre * sigmoid_value
    swish_ref[...] = swish_value
    slope_ref[...] = up_pre * (sigmoid_value * (1.0 + gate_pre * (1.0 - sigmoid_value)))
    hidden_ref[...] = swish_value * up_pre


def expert_kernel(count, lane_cap, *refs):
    parts = refs[:count]
    weight_ref, swish_ref, slope_ref, hidden_ref, out_ref = refs[count:]
    slots = parts[0].shape[0]
    columns = weight_ref.shape[0]
    grads, scores = [], []
    for at in range(count):
        pieces = []
        for step in range(count):
            source = (at - step) % count
            pieces.append(
                parts[step][:, source * TILE : (source + 1) * TILE].astype(jnp.float32)
            )
        back = cycle_sum(pieces)
        lanes = slice(at * TILE, (at + 1) * TILE)
        scores.append(hidden_ref[:, lanes] * back)
        grads.append((slope_ref[:, lanes] * back).astype(jnp.bfloat16))
        grads.append((swish_ref[:, lanes] * back).astype(jnp.bfloat16))
    total = nt(jnp.concatenate(grads, axis=1), weight_ref[...]).astype(jnp.bfloat16)
    lane_count = slots // lane_cap
    pieces = [
        total[:, first : first + TILE].reshape(lane_count, lane_cap, TILE)
        for first in range(0, columns, TILE)
    ]
    score = jnp.sum(cycle_sum(scores), axis=1, keepdims=True)
    lane = lax.rem(lax.axis_index("narrow"), lane_count // HALVES)
    slot, place = iota((slots, TILE), 0), iota((slots, TILE), 1)
    score = jnp.where(place == lane * lane_cap + slot % lane_cap, score, 0.0)
    score = jnp.sum(score.reshape(lane_count, lane_cap, TILE), axis=1, keepdims=True)
    pieces.append(jnp.broadcast_to(score, (lane_count, BLOCK, TILE)).astype(jnp.bfloat16))
    out_ref[...] = jnp.concatenate(pieces, axis=1)


def rows_kernel(group_cap, width, lane_cap, gated_ref, back_ref, out_ref):
    rows, columns = out_ref.shape
    gated = gated_ref[...]
    lane_count = back_ref.shape[0]
    pieces = [
        back_ref[:, tile * lane_cap : (tile + 1) * lane_cap, :].reshape(lane_count * lane_cap, TILE)
        for tile in range(columns // TILE)
    ]
    both = jnp.concatenate([gated, gated], axis=1)
    out_ref[...] = nn(both, jnp.concatenate(pieces, axis=1)).astype(jnp.bfloat16)
    score = back_ref[...][:, columns // TILE * lane_cap :, :].astype(jnp.float32)
    score = jnp.sum(jnp.sum(score, axis=0)[0:1, :], axis=0, keepdims=True)
    score = jnp.where(gated != 0, score, 0.0).astype(jnp.bfloat16)
    a, b = iota((rows, TILE), 0), iota((rows, TILE), 1)
    score = nn(score, bits(a // lane_cap == b % width))
    score = jnp.where(own_span(rows, width), score, 0.0).astype(jnp.bfloat16)
    notes = nn(spread(group_cap, rows), score)
    first = out_ref[:, 0:rows].astype(jnp.float32)
    out_ref[:, 0:rows] = (first + notes).astype(jnp.bfloat16)


def last_kernel(group_cap, width, ids_ref, place_ref, home_ref, tokens_ref, gates_ref):
    top, tokens = ids_ref.shape
    rows = home_ref.shape[0]
    ids = ids_ref[...]
    home = home_ref[...]
    place = jnp.transpose(place_ref[...].astype(jnp.float32)).astype(jnp.bfloat16)
    tokens_ref[...] = nn(place, home).astype(jnp.bfloat16)
    notes = nn(collect(group_cap, rows), home[:, 0:rows])
    notes = jnp.where(own_span(rows, width), notes, 0.0).astype(jnp.bfloat16)
    a, b = iota((rows, rows), 0), iota((rows, rows), 1)
    wide = nn(notes, bits((a % width == b % width) & (a < group_cap * width)))
    wide = jnp.where(a // BLOCK == b // width, wide, 0.0).astype(jnp.bfloat16)
    score = jnp.transpose(nn(place, wide))
    at = iota((rows, tokens), 0)
    for k in range(top):
        gates_ref[k : k + 1, :] = jnp.sum(
            jnp.where(ids[k : k + 1, :] == at, score, 0.0), axis=0, keepdims=True
        )


def exchange(values, axis):
    return lax.all_to_all(values, axis, split_axis=0, concat_axis=0, tiled=True)


def shift(values, step, count):
    return lax.ppermute(
        values, "tp", [(source, (source + step) % count) for source in range(count)]
    )


def shift_all(values):
    count = len(values)
    order = sorted(range(1, count), key=lambda step: min(step, count - step))
    moved = {step: shift(values[step], step, count) for step in order}
    return [values[0]] + [moved[step] for step in range(1, count)]


def per_device(d_out, expert_ids, gate_values, stored_preacts, w_gate, w_up, w_down):
    wide_count = lax.axis_size("wide")
    lane_count = lax.axis_size("narrow")
    split_count = lax.axis_size("tp")
    group_width = lane_count // HALVES
    token_count, model_width = d_out.shape
    slot_count = stored_preacts.shape[2]
    hidden_width = stored_preacts.shape[4]
    lane_cap = slot_count // lane_count
    group_cap = min(token_count, max(1, 3 * token_count * LIMIT // (2 * wide_count)))
    columns = model_width // split_count
    rows = wide_count * BLOCK
    lanes = group_width * lane_cap
    ids = expert_ids.T

    preacts = stored_preacts[0, 0].reshape(2 * slot_count, hidden_width)
    tiles = columns // TILE
    early_rows = tiles * hidden_width + 2 * slot_count
    others = split_count - 1
    send, place, *early = call(
        lambda *refs: first_kernel(group_cap, group_width, split_count, *refs),
        [shape(rows, columns), shape(rows, token_count)]
        + [shape(early_rows, hidden_width)] * others,
        (ids, gate_values.T, d_out, w_down[0, 0], preacts),
        spaces=[pltpu.HBM] * 5,
        out_spaces=[pltpu.VMEM] * (2 + others),
        vmem=60,
        scratch=[
            pltpu.VMEM(ids.shape, ids.dtype),
            pltpu.VMEM(ids.shape, gate_values.dtype),
            pltpu.VMEM((token_count, columns), d_out.dtype),
            pltpu.SemaphoreType.DMA((3 + others * (tiles + 1),)),
        ],
    )
    early = shift_all([None] + early)[1:]
    down_cols = call(
        join_kernel,
        shape(split_count * hidden_width, columns),
        (w_down[0, 0], *early),
        size=1 << 20,
        flops=18 * 10**9,
    )

    got = exchange(send.reshape(wide_count, BLOCK, columns), "wide").reshape(rows, columns)
    forward, gated = call(
        lambda *refs: second_kernel(group_cap, group_width, lane_cap, *refs),
        [shape(HALVES, lanes, columns), shape(rows, lanes)],
        (got,),
    )
    rest_packed = call(
        pack_rest_kernel,
        [shape(2 * columns, hidden_width)] * split_count,
        (
            w_gate[0, 0],
            w_up[0, 0],
            gated,
        ),
        size=4 << 20,
        spaces=[pltpu.VMEM] * 2 + [pl.ANY],
    )
    blocks = shift_all(rest_packed)
    slot_rows = exchange(forward.reshape(lane_count, lane_cap, columns), "narrow").reshape(
        slot_count, columns
    )
    partial = call(
        partial_kernel,
        shape(slot_count, split_count * hidden_width),
        (slot_rows, down_cols),
    )
    parts = shift_all([partial] * split_count)
    hidden_all = split_count * hidden_width
    prepared = call(
        lambda *refs: prepare_kernel(split_count, *refs),
        [shape(columns, 2 * hidden_all)]
        + [shape(slot_count, hidden_all, dtype=jnp.float32)] * 3,
        (preacts, *blocks, *early),
        size=8 << 20,
    )
    block_rows = columns // TILE * lane_cap + BLOCK
    terms = call(
        lambda *refs: expert_kernel(split_count, lane_cap, *refs),
        shape(lane_count, block_rows, TILE),
        (*parts, *prepared),
        vmem=24,
    )
    back = exchange(terms, "narrow")
    row_input = call(
        lambda *refs: rows_kernel(group_cap, group_width, lane_cap, *refs),
        shape(rows, columns),
        (gated, back),
    )
    home = exchange(row_input.reshape(wide_count, BLOCK, columns), "wide").reshape(rows, columns)
    d_tokens, d_gates = call(
        lambda *refs: last_kernel(group_cap, group_width, *refs),
        [
            shape(token_count, columns),
            shape(expert_ids.shape[1], token_count, dtype=jnp.float32),
        ],
        (ids, place, home),
    )
    return (d_tokens, d_gates.T)


def solution(mesh):
    return jax.shard_map(
        per_device,
        mesh=mesh,
        in_specs=(
            P(("wide", "narrow"), None),
            P(("wide", "narrow"), None),
            P(("wide", "narrow"), None),
            P("wide", "narrow", None, None, "tp"),
            P("wide", "narrow", None, "tp"),
            P("wide", "narrow", None, "tp"),
            P("wide", "narrow", "tp", None),
        ),
        out_specs=(P(("wide", "narrow"), "tp"), P(("wide", "narrow"), None)),
        check_vma=False,
    )
```

```python
import jax
import jax.numpy as jnp
from jax import lax
from jax.experimental import pallas as pl
from jax.experimental.pallas import tpu as pltpu
from jax.sharding import PartitionSpec as P

LIMIT = 4
HALVES = 2
BLOCK = 8
TILE = 128


def nn(left, right):
    return lax.dot_general(
        left, right, (((1,), (0,)), ((), ())), preferred_element_type=jnp.float32
    )


def nt(left, right):
    return lax.dot_general(
        left, right, (((1,), (1,)), ((), ())), preferred_element_type=jnp.float32
    )


def iota(shape, axis):
    return lax.broadcasted_iota(jnp.int32, shape, axis)


def bits(mask):
    return jnp.where(mask, 1.0, 0.0).astype(jnp.bfloat16)


def call(kernel, outs, args, flops=0, size=1 << 20, spaces=None, out_spaces=None, scratch=(), vmem=16):
    spaces = spaces or [pltpu.VMEM] * len(args)
    return pl.pallas_call(
        kernel,
        out_shape=outs,
        in_specs=[pl.BlockSpec(memory_space=space) for space in spaces],
        out_specs=[pl.BlockSpec(memory_space=space) for space in out_spaces]
        if out_spaces
        else jax.tree.map(lambda _: pl.BlockSpec(memory_space=pltpu.VMEM), outs),
        scratch_shapes=list(scratch),
        compiler_params=pltpu.CompilerParams(vmem_limit_bytes=vmem << 20),
        cost_estimate=pl.CostEstimate(flops=flops, bytes_accessed=size, transcendentals=0),
    )(*args)


def shape(*dims, dtype=jnp.bfloat16):
    return jax.ShapeDtypeStruct(dims, dtype)


def pack_rest_kernel(gate_ref, up_ref, after_ref, *out_refs):
    count = len(out_refs)
    width = gate_ref.shape[0] // count
    me = lax.axis_index("tp")
    for step, out_ref in enumerate(out_refs):
        to = lax.rem(me + step, count)
        rows = pl.ds(pl.multiple_of(to * width, TILE), width)
        out_ref[0:width, :] = gate_ref[rows, :]
        out_ref[width : 2 * width, :] = up_ref[rows, :]


def join_kernel(down_ref, *refs):
    block_refs, out_ref = by_step([down_ref, *refs[:-1]])[1:], refs[-1]
    hidden, columns = down_ref.shape[0], out_ref.shape[1]
    own = lax.axis_index("tp") * columns
    out_ref[0:hidden, :] = down_ref[:, pl.ds(pl.multiple_of(own, TILE), columns)]
    for at, block_ref in enumerate(block_refs, 1):
        for tile in range(columns // TILE):
            out_ref[at * hidden : (at + 1) * hidden, tile * TILE : (tile + 1) * TILE] = (
                block_ref[tile * hidden : (tile + 1) * hidden, :]
            )


def spread(group_cap, rows):
    r, c = iota((rows, rows), 0), iota((rows, rows), 1)
    return bits((r // BLOCK == c // BLOCK) & (r % BLOCK == group_cap))


def collect(group_cap, rows):
    r, c = iota((rows, rows), 0), iota((rows, rows), 1)
    return bits(
        (r // BLOCK == c // BLOCK) & (c % BLOCK == group_cap) & (r % BLOCK < group_cap)
    )


def own_span(rows, width):
    r, c = iota((rows, rows), 0), iota((rows, rows), 1)
    return c // width == r % BLOCK


def first_kernel(
    group_cap, width, count, ids_hbm, gates_hbm, rows_hbm, down_hbm, preacts_hbm, *refs
):
    send_ref, place_ref = refs[:2]
    block_hbms = refs[2 : 1 + count]
    ids_ref, gates_ref, rows_ref, block_refs, sems, out_sems = refs[1 + count :]
    columns = send_ref.shape[1]
    me = lax.axis_index("tp")

    def columns_of(index):
        return pl.ds(pl.multiple_of(index * columns, TILE), columns)

    loads = [
        pltpu.make_async_copy(ids_hbm, ids_ref, sems.at[0]),
        pltpu.make_async_copy(gates_hbm, gates_ref, sems.at[1]),
        pltpu.make_async_copy(rows_hbm.at[:, columns_of(me)], rows_ref, sems.at[2]),
    ]
    packs = []
    hidden = down_hbm.shape[0]
    for step in range(1, count):
        block_ref = block_refs.at[step - 1]
        first = lax.rem(me + step, count) * columns
        for tile in range(columns // TILE):
            lanes = pl.ds(pl.multiple_of(first + tile * TILE, TILE), TILE)
            packs.append((down_hbm.at[:, lanes], block_ref.at[pl.ds(tile * hidden, hidden)]))
        tail = pl.ds(columns // TILE * hidden, preacts_hbm.shape[0])
        packs.append((preacts_hbm, block_ref.at[tail]))
    packs = [
        pltpu.make_async_copy(source, target, sems.at[3 + at])
        for at, (source, target) in enumerate(packs)
    ]
    for copy in loads + packs:
        copy.start()
    for copy in loads:
        copy.wait()
    top, tokens = ids_ref.shape
    rows = send_ref.shape[0]
    groups = rows // BLOCK
    ids = ids_ref[...]
    gates = gates_ref[...].astype(jnp.float32)
    member = jnp.zeros((groups, tokens), jnp.float32)
    table = jnp.zeros((groups * width, tokens), jnp.float32)
    for k in range(top):
        one = ids[k : k + 1, :]
        member = jnp.where(one // width == iota((groups, tokens), 0), 1.0, member)
        table = jnp.where(one == iota((groups * width, tokens), 0), gates[k : k + 1, :], table)
    earlier = bits(iota((tokens, tokens), 0) < iota((tokens, tokens), 1))
    rank = nn(member.astype(jnp.bfloat16), earlier)
    rank = jnp.where((member > 0) & (rank < group_cap), rank, 100.0)
    grow = bits(iota((rows, groups), 0) // BLOCK == iota((rows, groups), 1))
    place = nn(grow, rank.astype(jnp.bfloat16)) == (
        iota((rows, tokens), 0) % BLOCK
    ).astype(jnp.float32)
    place = bits(place)
    place_ref[...] = place
    for copy in packs:
        copy.wait()
    stores = [
        pltpu.make_async_copy(block_refs.at[at], block_hbm, out_sems.at[at])
        for at, block_hbm in enumerate(block_hbms)
    ]
    for copy in stores:
        copy.start()
    send_ref[...] = nn(place, rows_ref[...]).astype(jnp.bfloat16)
    r, c = iota((rows, groups * width), 0), iota((rows, groups * width), 1)
    paired = nt(place, table.astype(jnp.bfloat16))
    paired = jnp.where(r // BLOCK == c // width, paired, 0.0).astype(jnp.bfloat16)
    a, b = iota((groups * width, rows), 0), iota((groups * width, rows), 1)
    repeated = nn(paired, bits(a % width == b % width))
    repeated = jnp.where(own_span(rows, width), repeated, 0.0).astype(jnp.bfloat16)
    notes = nn(spread(group_cap, rows), repeated)
    first = send_ref[:, 0:rows].astype(jnp.float32)
    send_ref[:, 0:rows] = (first + notes).astype(jnp.bfloat16)
    for copy in stores:
        copy.wait()


def second_kernel(group_cap, width, lane_cap, got_ref, *refs):
    out_ref, gated_ref = refs[-2:]
    rows = got_ref.shape[0]
    got = got_ref[...]
    notes = nn(collect(group_cap, rows), got[:, 0:rows])
    notes = jnp.where(own_span(rows, width), notes, 0.0).astype(jnp.bfloat16)
    slots = width * lane_cap
    a, b = iota((rows, slots), 0), iota((rows, slots), 1)
    gate = nn(notes, bits((a % width == b // lane_cap) & (a < group_cap * width)))
    hit = gate != 0.0
    rank = nn(bits(iota((rows, rows), 1) < iota((rows, rows), 0)), bits(hit))
    place = hit & (rank == (b % lane_cap).astype(jnp.float32))
    gated_ref[...] = jnp.where(place, gate, 0.0).astype(jnp.bfloat16)
    turned = jnp.transpose(jnp.where(place, 1.0, 0.0)).astype(jnp.bfloat16)
    moved = nn(turned, got).astype(jnp.bfloat16)
    for half in range(HALVES):
        out_ref[half] = moved


def partial_kernel(rows_ref, down_ref, out_ref):
    out_ref[...] = nt(rows_ref[...], down_ref[...]).astype(jnp.bfloat16)


def cycle_sum(terms):
    count = len(terms)
    while count > 1:
        count //= 2
        terms = [terms[i] + terms[i + count] for i in range(count)]
    return terms[0]


def prepare_kernel(count, preacts_ref, *refs):
    blocks = by_step(refs[:count])
    early = by_step([preacts_ref, *refs[count : 2 * count - 1]])
    weight_ref, swish_ref, slope_ref, hidden_ref = refs[2 * count - 1 :]
    columns = weight_ref.shape[0]
    slots = swish_ref.shape[0]
    for at, block_ref in enumerate(blocks):
        for part in range(2):
            first = (2 * at + part) * TILE
            weight_ref[:, first : first + TILE] = block_ref[part * columns : (part + 1) * columns, :]
    tail = early[1].shape[0] - 2 * slots
    raw = jnp.concatenate(
        [preacts_ref[...]] + [block_ref[tail:, :] for block_ref in early[1:]], axis=1
    )
    slot, row = iota((slots, 2 * slots), 0), iota((slots, 2 * slots), 1)
    gate_pre = nn(bits(row == 2 * slot), raw)
    up_pre = nn(bits(row == 2 * slot + 1), raw)
    sigmoid_value = jax.nn.sigmoid(gate_pre)
    swish_value = gate_pre * sigmoid_value
    swish_ref[...] = swish_value
    slope_ref[...] = up_pre * (sigmoid_value * (1.0 + gate_pre * (1.0 - sigmoid_value)))
    hidden_ref[...] = swish_value * up_pre


def expert_kernel(count, lane_cap, *refs):
    parts = by_step(refs[:count])
    weight_ref, swish_ref, slope_ref, hidden_ref, out_ref = refs[count:]
    slots = parts[0].shape[0]
    columns = weight_ref.shape[0]
    grads, scores = [], []
    for at in range(count):
        pieces = []
        for step in range(count):
            source = (at - step) % count
            pieces.append(
                parts[step][:, source * TILE : (source + 1) * TILE].astype(jnp.float32)
            )
        back = cycle_sum(pieces)
        lanes = slice(at * TILE, (at + 1) * TILE)
        scores.append(hidden_ref[:, lanes] * back)
        grads.append((slope_ref[:, lanes] * back).astype(jnp.bfloat16))
        grads.append((swish_ref[:, lanes] * back).astype(jnp.bfloat16))
    total = nt(jnp.concatenate(grads, axis=1), weight_ref[...]).astype(jnp.bfloat16)
    lane_count = slots // lane_cap
    pieces = [
        total[:, first : first + TILE].reshape(lane_count, lane_cap, TILE)
        for first in range(0, columns, TILE)
    ]
    score = jnp.sum(cycle_sum(scores), axis=1, keepdims=True)
    lane = lax.rem(lax.axis_index("narrow"), lane_count // HALVES)
    slot, place = iota((slots, TILE), 0), iota((slots, TILE), 1)
    score = jnp.where(place == lane * lane_cap + slot % lane_cap, score, 0.0)
    score = jnp.sum(score.reshape(lane_count, lane_cap, TILE), axis=1, keepdims=True)
    pieces.append(jnp.broadcast_to(score, (lane_count, BLOCK, TILE)).astype(jnp.bfloat16))
    out_ref[...] = jnp.concatenate(pieces, axis=1)


def rows_kernel(group_cap, width, lane_cap, gated_ref, back_ref, out_ref):
    rows, columns = out_ref.shape
    gated = gated_ref[...]
    lane_count = back_ref.shape[0]
    pieces = [
        back_ref[:, tile * lane_cap : (tile + 1) * lane_cap, :].reshape(lane_count * lane_cap, TILE)
        for tile in range(columns // TILE)
    ]
    both = jnp.concatenate([gated, gated], axis=1)
    out_ref[...] = nn(both, jnp.concatenate(pieces, axis=1)).astype(jnp.bfloat16)
    score = back_ref[...][:, columns // TILE * lane_cap :, :].astype(jnp.float32)
    score = jnp.sum(jnp.sum(score, axis=0)[0:1, :], axis=0, keepdims=True)
    score = jnp.where(gated != 0, score, 0.0).astype(jnp.bfloat16)
    a, b = iota((rows, TILE), 0), iota((rows, TILE), 1)
    score = nn(score, bits(a // lane_cap == b % width))
    score = jnp.where(own_span(rows, width), score, 0.0).astype(jnp.bfloat16)
    notes = nn(spread(group_cap, rows), score)
    first = out_ref[:, 0:rows].astype(jnp.float32)
    out_ref[:, 0:rows] = (first + notes).astype(jnp.bfloat16)


def last_kernel(group_cap, width, ids_ref, place_ref, home_ref, tokens_ref, gates_ref):
    top, tokens = ids_ref.shape
    rows = home_ref.shape[0]
    ids = ids_ref[...]
    home = home_ref[...]
    place = jnp.transpose(place_ref[...].astype(jnp.float32)).astype(jnp.bfloat16)
    tokens_ref[...] = nn(place, home).astype(jnp.bfloat16)
    notes = nn(collect(group_cap, rows), home[:, 0:rows])
    notes = jnp.where(own_span(rows, width), notes, 0.0).astype(jnp.bfloat16)
    a, b = iota((rows, rows), 0), iota((rows, rows), 1)
    wide = nn(notes, bits((a % width == b % width) & (a < group_cap * width)))
    wide = jnp.where(a // BLOCK == b // width, wide, 0.0).astype(jnp.bfloat16)
    score = jnp.transpose(nn(place, wide))
    at = iota((rows, tokens), 0)
    for k in range(top):
        gates_ref[k : k + 1, :] = jnp.sum(
            jnp.where(ids[k : k + 1, :] == at, score, 0.0), axis=0, keepdims=True
        )


def exchange(values, axis):
    return lax.all_to_all(values, axis, split_axis=0, concat_axis=0, tiled=True)


def shift(values, step, count):
    return lax.ppermute(
        values, "tp", [(source, (source + step) % count) for source in range(count)]
    )


def far_first(count):
    return [0] + sorted(range(1, count), key=lambda step: -min(step, count - step))


def by_step(values):
    order = far_first(len(values))
    return [values[order.index(step)] for step in range(len(values))]


def shift_all(values):
    count = len(values)
    return [values[0]] + [shift(values[step], step, count) for step in range(1, count)]


def per_device(d_out, expert_ids, gate_values, stored_preacts, w_gate, w_up, w_down):
    wide_count = lax.axis_size("wide")
    lane_count = lax.axis_size("narrow")
    split_count = lax.axis_size("tp")
    group_width = lane_count // HALVES
    token_count, model_width = d_out.shape
    slot_count = stored_preacts.shape[2]
    hidden_width = stored_preacts.shape[4]
    lane_cap = slot_count // lane_count
    group_cap = min(token_count, max(1, 3 * token_count * LIMIT // (2 * wide_count)))
    columns = model_width // split_count
    rows = wide_count * BLOCK
    lanes = group_width * lane_cap
    ids = expert_ids.T

    preacts = stored_preacts[0, 0].reshape(2 * slot_count, hidden_width)
    tiles = columns // TILE
    early_rows = tiles * hidden_width + 2 * slot_count
    others = split_count - 1
    send, place, *early = call(
        lambda *refs: first_kernel(group_cap, group_width, split_count, *refs),
        [shape(rows, columns), shape(rows, token_count)]
        + [shape(early_rows, hidden_width)] * others,
        (ids, gate_values.T, d_out, w_down[0, 0], preacts),
        spaces=[pltpu.HBM] * 5,
        out_spaces=[pltpu.VMEM] * 2 + [pltpu.HBM] * others,
        vmem=60,
        scratch=[
            pltpu.VMEM(ids.shape, ids.dtype),
            pltpu.VMEM(ids.shape, gate_values.dtype),
            pltpu.VMEM((token_count, columns), d_out.dtype),
            pltpu.VMEM((others, early_rows, hidden_width), d_out.dtype),
            pltpu.SemaphoreType.DMA((3 + others * (tiles + 1),)),
            pltpu.SemaphoreType.DMA((others,)),
        ],
    )
    early = shift_all([None] + early)
    early = [early[step] for step in far_first(split_count)[1:]]
    down_cols = call(
        join_kernel,
        shape(split_count * hidden_width, columns),
        (w_down[0, 0], *early),
        size=1 << 20,
        flops=18 * 10**9,
    )

    got = exchange(send.reshape(wide_count, BLOCK, columns), "wide").reshape(rows, columns)
    forward, gated = call(
        lambda *refs: second_kernel(group_cap, group_width, lane_cap, *refs),
        [shape(HALVES, lanes, columns), shape(rows, lanes)],
        (got,),
    )
    rest_packed = call(
        pack_rest_kernel,
        [shape(2 * columns, hidden_width)] * split_count,
        (
            w_gate[0, 0],
            w_up[0, 0],
            gated,
        ),
        size=4 << 20,
        spaces=[pltpu.VMEM] * 2 + [pl.ANY],
    )
    blocks = shift_all(rest_packed)
    slot_rows = exchange(forward.reshape(lane_count, lane_cap, columns), "narrow").reshape(
        slot_count, columns
    )
    partial = call(
        partial_kernel,
        shape(slot_count, split_count * hidden_width),
        (slot_rows, down_cols),
    )
    parts = shift_all([partial] * split_count)
    hidden_all = split_count * hidden_width
    prepared = call(
        lambda *refs: prepare_kernel(split_count, *refs),
        [shape(columns, 2 * hidden_all)]
        + [shape(slot_count, hidden_all, dtype=jnp.float32)] * 3,
        (preacts, *(blocks[step] for step in far_first(split_count)), *early),
        size=8 << 20,
    )
    block_rows = columns // TILE * lane_cap + BLOCK
    terms = call(
        lambda *refs: expert_kernel(split_count, lane_cap, *refs),
        shape(lane_count, block_rows, TILE),
        (*(parts[step] for step in far_first(split_count)), *prepared),
        vmem=24,
    )
    back = exchange(terms, "narrow")
    row_input = call(
        lambda *refs: rows_kernel(group_cap, group_width, lane_cap, *refs),
        shape(rows, columns),
        (gated, back),
    )
    home = exchange(row_input.reshape(wide_count, BLOCK, columns), "wide").reshape(rows, columns)
    d_tokens, d_gates = call(
        lambda *refs: last_kernel(group_cap, group_width, *refs),
        [
            shape(token_count, columns),
            shape(expert_ids.shape[1], token_count, dtype=jnp.float32),
        ],
        (ids, place, home),
    )
    return (d_tokens, d_gates.T)


def solution(mesh):
    return jax.shard_map(
        per_device,
        mesh=mesh,
        in_specs=(
            P(("wide", "narrow"), None),
            P(("wide", "narrow"), None),
            P(("wide", "narrow"), None),
            P("wide", "narrow", None, None, "tp"),
            P("wide", "narrow", None, "tp"),
            P("wide", "narrow", None, "tp"),
            P("wide", "narrow", "tp", None),
        ),
        out_specs=(P(("wide", "narrow"), "tp"), P(("wide", "narrow"), None)),
        check_vma=False,
    )
```

```python
import jax
import jax.numpy as jnp
from jax import lax
from jax.experimental import pallas as pl
from jax.experimental.pallas import tpu as pltpu
from jax.sharding import PartitionSpec as P

LIMIT = 4
HALVES = 2
BLOCK = 8
TILE = 128


def nn(left, right):
    return lax.dot_general(
        left, right, (((1,), (0,)), ((), ())), preferred_element_type=jnp.float32
    )


def nt(left, right):
    return lax.dot_general(
        left, right, (((1,), (1,)), ((), ())), preferred_element_type=jnp.float32
    )


def iota(shape, axis):
    return lax.broadcasted_iota(jnp.int32, shape, axis)


def bits(mask):
    return jnp.where(mask, 1.0, 0.0).astype(jnp.bfloat16)


def call(kernel, outs, args, flops=0, size=1 << 20, spaces=None, out_spaces=None, scratch=(), vmem=16):
    spaces = spaces or [pltpu.VMEM] * len(args)
    return pl.pallas_call(
        kernel,
        out_shape=outs,
        in_specs=[pl.BlockSpec(memory_space=space) for space in spaces],
        out_specs=[pl.BlockSpec(memory_space=space) for space in out_spaces]
        if out_spaces
        else jax.tree.map(lambda _: pl.BlockSpec(memory_space=pltpu.VMEM), outs),
        scratch_shapes=list(scratch),
        compiler_params=pltpu.CompilerParams(vmem_limit_bytes=vmem << 20),
        cost_estimate=pl.CostEstimate(flops=flops, bytes_accessed=size, transcendentals=0),
    )(*args)


def shape(*dims, dtype=jnp.bfloat16):
    return jax.ShapeDtypeStruct(dims, dtype)


def pack_rest_kernel(gate_ref, up_ref, after_ref, *out_refs):
    count = len(out_refs) + 1
    width = gate_ref.shape[0] // count
    me = lax.axis_index("tp")
    for step, out_ref in enumerate(out_refs, 1):
        to = lax.rem(me + step, count)
        rows = pl.ds(pl.multiple_of(to * width, TILE), width)
        out_ref[0:width, :] = gate_ref[rows, :]
        out_ref[width : 2 * width, :] = up_ref[rows, :]


def join_kernel(down_ref, *refs):
    block_refs, out_ref = by_step([down_ref, *refs[:-1]])[1:], refs[-1]
    hidden, columns = down_ref.shape[0], out_ref.shape[1]
    own = lax.axis_index("tp") * columns
    out_ref[0:hidden, :] = down_ref[:, pl.ds(pl.multiple_of(own, TILE), columns)]
    for at, block_ref in enumerate(block_refs, 1):
        for tile in range(columns // TILE):
            out_ref[at * hidden : (at + 1) * hidden, tile * TILE : (tile + 1) * TILE] = (
                block_ref[tile * hidden : (tile + 1) * hidden, :]
            )


def spread(group_cap, rows):
    r, c = iota((rows, rows), 0), iota((rows, rows), 1)
    return bits((r // BLOCK == c // BLOCK) & (r % BLOCK == group_cap))


def collect(group_cap, rows):
    r, c = iota((rows, rows), 0), iota((rows, rows), 1)
    return bits(
        (r // BLOCK == c // BLOCK) & (c % BLOCK == group_cap) & (r % BLOCK < group_cap)
    )


def own_span(rows, width):
    r, c = iota((rows, rows), 0), iota((rows, rows), 1)
    return c // width == r % BLOCK


def first_kernel(
    group_cap, width, count, ids_hbm, gates_hbm, rows_hbm, down_hbm, preacts_hbm, *refs
):
    send_ref, place_ref = refs[:2]
    block_hbms = refs[2 : 1 + count]
    ids_ref, gates_ref, rows_ref, down_ref, block_refs, sems, out_sems = refs[1 + count :]
    columns = send_ref.shape[1]
    me = lax.axis_index("tp")

    def columns_of(index):
        return pl.ds(pl.multiple_of(index * columns, TILE), columns)

    loads = [
        pltpu.make_async_copy(ids_hbm, ids_ref, sems.at[0]),
        pltpu.make_async_copy(gates_hbm, gates_ref, sems.at[1]),
        pltpu.make_async_copy(rows_hbm.at[:, columns_of(me)], rows_ref, sems.at[2]),
    ]
    hidden = down_hbm.shape[0]
    tiles = columns // TILE
    tail = pl.ds(tiles * hidden, preacts_hbm.shape[0])
    packs = [pltpu.make_async_copy(down_hbm, down_ref, sems.at[3])] + [
        pltpu.make_async_copy(preacts_hbm, block_refs.at[at, tail], sems.at[4 + at])
        for at in range(count - 1)
    ]
    for copy in loads + packs:
        copy.start()
    for copy in loads:
        copy.wait()
    top, tokens = ids_ref.shape
    rows = send_ref.shape[0]
    groups = rows // BLOCK
    ids = ids_ref[...]
    gates = gates_ref[...].astype(jnp.float32)
    member = jnp.zeros((groups, tokens), jnp.float32)
    table = jnp.zeros((groups * width, tokens), jnp.float32)
    for k in range(top):
        one = ids[k : k + 1, :]
        member = jnp.where(one // width == iota((groups, tokens), 0), 1.0, member)
        table = jnp.where(one == iota((groups * width, tokens), 0), gates[k : k + 1, :], table)
    earlier = bits(iota((tokens, tokens), 0) < iota((tokens, tokens), 1))
    rank = nn(member.astype(jnp.bfloat16), earlier)
    rank = jnp.where((member > 0) & (rank < group_cap), rank, 100.0)
    grow = bits(iota((rows, groups), 0) // BLOCK == iota((rows, groups), 1))
    place = nn(grow, rank.astype(jnp.bfloat16)) == (
        iota((rows, tokens), 0) % BLOCK
    ).astype(jnp.float32)
    place = bits(place)
    place_ref[...] = place
    for copy in packs:
        copy.wait()
    for step in range(1, count):
        begin = lax.rem(me + step, count) * columns
        for tile in range(tiles):
            lanes = pl.ds(pl.multiple_of(begin + tile * TILE, TILE), TILE)
            block_refs[step - 1, tile * hidden : (tile + 1) * hidden, :] = down_ref[:, lanes]
    stores = [
        pltpu.make_async_copy(block_refs.at[at], block_hbm, out_sems.at[at])
        for at, block_hbm in enumerate(block_hbms)
    ]
    for copy in stores:
        copy.start()
    send_ref[...] = nn(place, rows_ref[...]).astype(jnp.bfloat16)
    r, c = iota((rows, groups * width), 0), iota((rows, groups * width), 1)
    paired = nt(place, table.astype(jnp.bfloat16))
    paired = jnp.where(r // BLOCK == c // width, paired, 0.0).astype(jnp.bfloat16)
    a, b = iota((groups * width, rows), 0), iota((groups * width, rows), 1)
    repeated = nn(paired, bits(a % width == b % width))
    repeated = jnp.where(own_span(rows, width), repeated, 0.0).astype(jnp.bfloat16)
    notes = nn(spread(group_cap, rows), repeated)
    first = send_ref[:, 0:rows].astype(jnp.float32)
    send_ref[:, 0:rows] = (first + notes).astype(jnp.bfloat16)
    for copy in stores:
        copy.wait()


def second_kernel(group_cap, width, lane_cap, got_ref, *refs):
    out_ref, gated_ref = refs[-2:]
    rows = got_ref.shape[0]
    got = got_ref[...]
    notes = nn(collect(group_cap, rows), got[:, 0:rows])
    notes = jnp.where(own_span(rows, width), notes, 0.0).astype(jnp.bfloat16)
    slots = width * lane_cap
    a, b = iota((rows, slots), 0), iota((rows, slots), 1)
    gate = nn(notes, bits((a % width == b // lane_cap) & (a < group_cap * width)))
    hit = gate != 0.0
    rank = nn(bits(iota((rows, rows), 1) < iota((rows, rows), 0)), bits(hit))
    place = hit & (rank == (b % lane_cap).astype(jnp.float32))
    gated_ref[...] = jnp.where(place, gate, 0.0).astype(jnp.bfloat16)
    turned = jnp.transpose(jnp.where(place, 1.0, 0.0)).astype(jnp.bfloat16)
    moved = nn(turned, got).astype(jnp.bfloat16)
    for half in range(HALVES):
        out_ref[half] = moved


def partial_kernel(rows_ref, down_ref, out_ref):
    out_ref[...] = nt(rows_ref[...], down_ref[...]).astype(jnp.bfloat16)


def cycle_sum(terms):
    count = len(terms)
    while count > 1:
        count //= 2
        terms = [terms[i] + terms[i + count] for i in range(count)]
    return terms[0]


def prepare_kernel(count, preacts_ref, gate_hbm, up_hbm, *refs):
    blocks = by_step([None, *refs[: count - 1]])
    early = by_step([preacts_ref, *refs[count - 1 : 2 * count - 2]])
    weight_ref, swish_ref, slope_ref, hidden_ref, own_ref, sems = refs[2 * count - 2 :]
    columns = weight_ref.shape[0]
    slots = swish_ref.shape[0]
    own = pl.ds(pl.multiple_of(lax.axis_index("tp") * columns, TILE), columns)
    copies = [
        pltpu.make_async_copy(source.at[own], own_ref.at[part], sems.at[part])
        for part, source in enumerate((gate_hbm, up_hbm))
    ]
    for copy in copies:
        copy.start()
    for at, block_ref in enumerate(blocks[1:], 1):
        for part in range(2):
            first = (2 * at + part) * TILE
            weight_ref[:, first : first + TILE] = block_ref[part * columns : (part + 1) * columns, :]
    tail = early[1].shape[0] - 2 * slots
    raw = jnp.concatenate(
        [preacts_ref[...]] + [block_ref[tail:, :] for block_ref in early[1:]], axis=1
    )
    slot, row = iota((slots, 2 * slots), 0), iota((slots, 2 * slots), 1)
    gate_pre = nn(bits(row == 2 * slot), raw)
    up_pre = nn(bits(row == 2 * slot + 1), raw)
    sigmoid_value = jax.nn.sigmoid(gate_pre)
    swish_value = gate_pre * sigmoid_value
    swish_ref[...] = swish_value
    slope_ref[...] = up_pre * (sigmoid_value * (1.0 + gate_pre * (1.0 - sigmoid_value)))
    hidden_ref[...] = swish_value * up_pre
    for part, copy in enumerate(copies):
        copy.wait()
        weight_ref[:, part * TILE : (part + 1) * TILE] = own_ref[part]


def expert_kernel(count, lane_cap, *refs):
    parts = by_step(refs[:count])
    weight_ref, swish_ref, slope_ref, hidden_ref, out_ref = refs[count:]
    slots = parts[0].shape[0]
    columns = weight_ref.shape[0]
    grads, scores = [], []
    for at in range(count):
        pieces = []
        for step in range(count):
            source = (at - step) % count
            pieces.append(
                parts[step][:, source * TILE : (source + 1) * TILE].astype(jnp.float32)
            )
        back = cycle_sum(pieces)
        lanes = slice(at * TILE, (at + 1) * TILE)
        scores.append(hidden_ref[:, lanes] * back)
        grads.append((slope_ref[:, lanes] * back).astype(jnp.bfloat16))
        grads.append((swish_ref[:, lanes] * back).astype(jnp.bfloat16))
    total = nt(jnp.concatenate(grads, axis=1), weight_ref[...]).astype(jnp.bfloat16)
    lane_count = slots // lane_cap
    pieces = [
        total[:, first : first + TILE].reshape(lane_count, lane_cap, TILE)
        for first in range(0, columns, TILE)
    ]
    score = jnp.sum(cycle_sum(scores), axis=1, keepdims=True)
    lane = lax.rem(lax.axis_index("narrow"), lane_count // HALVES)
    slot, place = iota((slots, TILE), 0), iota((slots, TILE), 1)
    score = jnp.where(place == lane * lane_cap + slot % lane_cap, score, 0.0)
    score = jnp.sum(score.reshape(lane_count, lane_cap, TILE), axis=1, keepdims=True)
    pieces.append(jnp.broadcast_to(score, (lane_count, BLOCK, TILE)).astype(jnp.bfloat16))
    out_ref[...] = jnp.concatenate(pieces, axis=1)


def rows_kernel(group_cap, width, lane_cap, gated_ref, back_ref, out_ref):
    rows, columns = out_ref.shape
    gated = gated_ref[...]
    lane_count = back_ref.shape[0]
    pieces = [
        back_ref[:, tile * lane_cap : (tile + 1) * lane_cap, :].reshape(lane_count * lane_cap, TILE)
        for tile in range(columns // TILE)
    ]
    both = jnp.concatenate([gated, gated], axis=1)
    out_ref[...] = nn(both, jnp.concatenate(pieces, axis=1)).astype(jnp.bfloat16)
    score = back_ref[...][:, columns // TILE * lane_cap :, :].astype(jnp.float32)
    score = jnp.sum(jnp.sum(score, axis=0)[0:1, :], axis=0, keepdims=True)
    score = jnp.where(gated != 0, score, 0.0).astype(jnp.bfloat16)
    a, b = iota((rows, TILE), 0), iota((rows, TILE), 1)
    score = nn(score, bits(a // lane_cap == b % width))
    score = jnp.where(own_span(rows, width), score, 0.0).astype(jnp.bfloat16)
    notes = nn(spread(group_cap, rows), score)
    first = out_ref[:, 0:rows].astype(jnp.float32)
    out_ref[:, 0:rows] = (first + notes).astype(jnp.bfloat16)


def last_kernel(group_cap, width, ids_ref, place_ref, home_ref, tokens_ref, gates_ref):
    top, tokens = ids_ref.shape
    rows = home_ref.shape[0]
    ids = ids_ref[...]
    home = home_ref[...]
    place = jnp.transpose(place_ref[...].astype(jnp.float32)).astype(jnp.bfloat16)
    tokens_ref[...] = nn(place, home).astype(jnp.bfloat16)
    notes = nn(collect(group_cap, rows), home[:, 0:rows])
    notes = jnp.where(own_span(rows, width), notes, 0.0).astype(jnp.bfloat16)
    a, b = iota((rows, rows), 0), iota((rows, rows), 1)
    wide = nn(notes, bits((a % width == b % width) & (a < group_cap * width)))
    wide = jnp.where(a // BLOCK == b // width, wide, 0.0).astype(jnp.bfloat16)
    score = jnp.transpose(nn(place, wide))
    at = iota((rows, tokens), 0)
    for k in range(top):
        gates_ref[k : k + 1, :] = jnp.sum(
            jnp.where(ids[k : k + 1, :] == at, score, 0.0), axis=0, keepdims=True
        )


def exchange(values, axis):
    return lax.all_to_all(values, axis, split_axis=0, concat_axis=0, tiled=True)


def shift(values, step, count):
    return lax.ppermute(
        values, "tp", [(source, (source + step) % count) for source in range(count)]
    )


def far_first(count):
    return [0] + sorted(range(1, count), key=lambda step: -min(step, count - step))


def by_step(values):
    order = far_first(len(values))
    return [values[order.index(step)] for step in range(len(values))]


def shift_all(values):
    count = len(values)
    return [values[0]] + [shift(values[step], step, count) for step in range(1, count)]


def per_device(d_out, expert_ids, gate_values, stored_preacts, w_gate, w_up, w_down):
    wide_count = lax.axis_size("wide")
    lane_count = lax.axis_size("narrow")
    split_count = lax.axis_size("tp")
    group_width = lane_count // HALVES
    token_count, model_width = d_out.shape
    slot_count = stored_preacts.shape[2]
    hidden_width = stored_preacts.shape[4]
    lane_cap = slot_count // lane_count
    group_cap = min(token_count, max(1, 3 * token_count * LIMIT // (2 * wide_count)))
    columns = model_width // split_count
    rows = wide_count * BLOCK
    lanes = group_width * lane_cap
    ids = expert_ids.T

    preacts = stored_preacts[0, 0].reshape(2 * slot_count, hidden_width)
    tiles = columns // TILE
    early_rows = tiles * hidden_width + 2 * slot_count
    others = split_count - 1
    send, place, *early = call(
        lambda *refs: first_kernel(group_cap, group_width, split_count, *refs),
        [shape(rows, columns), shape(rows, token_count)]
        + [shape(early_rows, hidden_width)] * others,
        (ids, gate_values.T, d_out, w_down[0, 0], preacts),
        spaces=[pltpu.HBM] * 5,
        out_spaces=[pltpu.VMEM] * 2 + [pltpu.HBM] * others,
        vmem=60,
        scratch=[
            pltpu.VMEM(ids.shape, ids.dtype),
            pltpu.VMEM(ids.shape, gate_values.dtype),
            pltpu.VMEM((token_count, columns), d_out.dtype),
            pltpu.VMEM((hidden_width, model_width), d_out.dtype),
            pltpu.VMEM((others, early_rows, hidden_width), d_out.dtype),
            pltpu.SemaphoreType.DMA((4 + others,)),
            pltpu.SemaphoreType.DMA((others,)),
        ],
    )
    early = shift_all([None] + early)
    early = [early[step] for step in far_first(split_count)[1:]]
    down_cols = call(
        join_kernel,
        shape(split_count * hidden_width, columns),
        (w_down[0, 0], *early),
        size=1 << 20,
        flops=18 * 10**9,
    )

    got = exchange(send.reshape(wide_count, BLOCK, columns), "wide").reshape(rows, columns)
    forward, gated = call(
        lambda *refs: second_kernel(group_cap, group_width, lane_cap, *refs),
        [shape(HALVES, lanes, columns), shape(rows, lanes)],
        (got,),
    )
    rest_packed = call(
        pack_rest_kernel,
        [shape(2 * columns, hidden_width)] * others,
        (
            w_gate[0, 0],
            w_up[0, 0],
            gated,
        ),
        size=4 << 20,
        spaces=[pltpu.VMEM] * 2 + [pl.ANY],
    )
    blocks = shift_all([None, *rest_packed])
    slot_rows = exchange(forward.reshape(lane_count, lane_cap, columns), "narrow").reshape(
        slot_count, columns
    )
    partial = call(
        partial_kernel,
        shape(slot_count, split_count * hidden_width),
        (slot_rows, down_cols),
    )
    parts = shift_all([partial] * split_count)
    hidden_all = split_count * hidden_width
    prepared = call(
        lambda *refs: prepare_kernel(split_count, *refs),
        [shape(columns, 2 * hidden_all)]
        + [shape(slot_count, hidden_all, dtype=jnp.float32)] * 3,
        (
            preacts,
            w_gate[0, 0],
            w_up[0, 0],
            *(blocks[step] for step in far_first(split_count)[1:]),
            *early,
        ),
        spaces=[pltpu.VMEM] + [pl.ANY] * 2 + [pltpu.VMEM] * (2 * others),
        scratch=[
            pltpu.VMEM((2, columns, hidden_width), w_gate.dtype),
            pltpu.SemaphoreType.DMA((2,)),
        ],
        size=8 << 20,
    )
    block_rows = columns // TILE * lane_cap + BLOCK
    terms = call(
        lambda *refs: expert_kernel(split_count, lane_cap, *refs),
        shape(lane_count, block_rows, TILE),
        (*(parts[step] for step in far_first(split_count)), *prepared),
        vmem=24,
    )
    back = exchange(terms, "narrow")
    row_input = call(
        lambda *refs: rows_kernel(group_cap, group_width, lane_cap, *refs),
        shape(rows, columns),
        (gated, back),
    )
    home = exchange(row_input.reshape(wide_count, BLOCK, columns), "wide").reshape(rows, columns)
    d_tokens, d_gates = call(
        lambda *refs: last_kernel(group_cap, group_width, *refs),
        [
            shape(token_count, columns),
            shape(expert_ids.shape[1], token_count, dtype=jnp.float32),
        ],
        (ids, place, home),
    )
    return (d_tokens, d_gates.T)


def solution(mesh):
    return jax.shard_map(
        per_device,
        mesh=mesh,
        in_specs=(
            P(("wide", "narrow"), None),
            P(("wide", "narrow"), None),
            P(("wide", "narrow"), None),
            P("wide", "narrow", None, None, "tp"),
            P("wide", "narrow", None, "tp"),
            P("wide", "narrow", None, "tp"),
            P("wide", "narrow", "tp", None),
        ),
        out_specs=(P(("wide", "narrow"), "tp"), P(("wide", "narrow"), None)),
        check_vma=False,
    )
```

```python
import jax
import jax.numpy as jnp
from jax import lax
from jax.experimental import pallas as pl
from jax.experimental.pallas import tpu as pltpu
from jax.sharding import PartitionSpec as P

LIMIT = 4
HALVES = 2
BLOCK = 8
TILE = 128


def nn(left, right):
    return lax.dot_general(
        left, right, (((1,), (0,)), ((), ())), preferred_element_type=jnp.float32
    )


def nt(left, right):
    return lax.dot_general(
        left, right, (((1,), (1,)), ((), ())), preferred_element_type=jnp.float32
    )


def iota(shape, axis):
    return lax.broadcasted_iota(jnp.int32, shape, axis)


def bits(mask):
    return jnp.where(mask, 1.0, 0.0).astype(jnp.bfloat16)


def call(kernel, outs, args, flops=0, size=1 << 20, spaces=None, out_spaces=None, scratch=(), vmem=16):
    spaces = spaces or [pltpu.VMEM] * len(args)
    return pl.pallas_call(
        kernel,
        out_shape=outs,
        in_specs=[pl.BlockSpec(memory_space=space) for space in spaces],
        out_specs=[pl.BlockSpec(memory_space=space) for space in out_spaces]
        if out_spaces
        else jax.tree.map(lambda _: pl.BlockSpec(memory_space=pltpu.VMEM), outs),
        scratch_shapes=list(scratch),
        compiler_params=pltpu.CompilerParams(vmem_limit_bytes=vmem << 20),
        cost_estimate=pl.CostEstimate(flops=flops, bytes_accessed=size, transcendentals=0),
    )(*args)


def shape(*dims, dtype=jnp.bfloat16):
    return jax.ShapeDtypeStruct(dims, dtype)


def pack_rest_kernel(gate_ref, up_ref, after_ref, *out_refs):
    count = len(out_refs)
    width = gate_ref.shape[0] // count
    me = lax.axis_index("tp")
    for step, out_ref in enumerate(out_refs):
        to = lax.rem(me + step, count)
        rows = pl.ds(pl.multiple_of(to * width, TILE), width)
        out_ref[0:width, :] = gate_ref[rows, :]
        out_ref[width : 2 * width, :] = up_ref[rows, :]


def join_kernel(down_ref, *refs):
    block_refs, out_ref = by_step([down_ref, *refs[:-1]])[1:], refs[-1]
    hidden, columns = down_ref.shape[0], out_ref.shape[1]
    own = lax.axis_index("tp") * columns
    out_ref[0:hidden, :] = down_ref[:, pl.ds(pl.multiple_of(own, TILE), columns)]
    for at, block_ref in enumerate(block_refs, 1):
        for tile in range(columns // TILE):
            out_ref[at * hidden : (at + 1) * hidden, tile * TILE : (tile + 1) * TILE] = (
                block_ref[tile * hidden : (tile + 1) * hidden, :]
            )


def spread(group_cap, rows):
    r, c = iota((rows, rows), 0), iota((rows, rows), 1)
    return bits((r // BLOCK == c // BLOCK) & (r % BLOCK == group_cap))


def collect(group_cap, rows):
    r, c = iota((rows, rows), 0), iota((rows, rows), 1)
    return bits(
        (r // BLOCK == c // BLOCK) & (c % BLOCK == group_cap) & (r % BLOCK < group_cap)
    )


def own_span(rows, width):
    r, c = iota((rows, rows), 0), iota((rows, rows), 1)
    return c // width == r % BLOCK


def first_kernel(
    group_cap, width, count, ids_hbm, gates_hbm, rows_hbm, down_hbm, preacts_hbm, *refs
):
    send_ref, place_ref = refs[:2]
    block_refs = refs[2 : 1 + count]
    ids_ref, gates_ref, rows_ref, sems = refs[1 + count :]
    columns = send_ref.shape[1]
    me = lax.axis_index("tp")

    def columns_of(index):
        return pl.ds(pl.multiple_of(index * columns, TILE), columns)

    loads = [
        pltpu.make_async_copy(ids_hbm, ids_ref, sems.at[0]),
        pltpu.make_async_copy(gates_hbm, gates_ref, sems.at[1]),
        pltpu.make_async_copy(rows_hbm.at[:, columns_of(me)], rows_ref, sems.at[2]),
    ]
    packs = []
    hidden = down_hbm.shape[0]
    for step, block_ref in enumerate(block_refs, 1):
        first = lax.rem(me + step, count) * columns
        for tile in range(columns // TILE):
            lanes = pl.ds(pl.multiple_of(first + tile * TILE, TILE), TILE)
            packs.append((down_hbm.at[:, lanes], block_ref.at[pl.ds(tile * hidden, hidden)]))
        tail = pl.ds(columns // TILE * hidden, preacts_hbm.shape[0])
        packs.append((preacts_hbm, block_ref.at[tail]))
    packs = [
        pltpu.make_async_copy(source, target, sems.at[3 + at])
        for at, (source, target) in enumerate(packs)
    ]
    for copy in loads + packs:
        copy.start()
    for copy in loads:
        copy.wait()
    top, tokens = ids_ref.shape
    rows = send_ref.shape[0]
    groups = rows // BLOCK
    ids = ids_ref[...]
    gates = gates_ref[...].astype(jnp.float32)
    member = jnp.zeros((groups, tokens), jnp.float32)
    table = jnp.zeros((groups * width, tokens), jnp.float32)
    for k in range(top):
        one = ids[k : k + 1, :]
        member = jnp.where(one // width == iota((groups, tokens), 0), 1.0, member)
        table = jnp.where(one == iota((groups * width, tokens), 0), gates[k : k + 1, :], table)
    earlier = bits(iota((tokens, tokens), 0) < iota((tokens, tokens), 1))
    rank = nn(member.astype(jnp.bfloat16), earlier)
    rank = jnp.where((member > 0) & (rank < group_cap), rank, 100.0)
    grow = bits(iota((rows, groups), 0) // BLOCK == iota((rows, groups), 1))
    place = nn(grow, rank.astype(jnp.bfloat16)) == (
        iota((rows, tokens), 0) % BLOCK
    ).astype(jnp.float32)
    place = bits(place)
    place_ref[...] = place
    send_ref[...] = nn(place, rows_ref[...]).astype(jnp.bfloat16)
    r, c = iota((rows, groups * width), 0), iota((rows, groups * width), 1)
    paired = nt(place, table.astype(jnp.bfloat16))
    paired = jnp.where(r // BLOCK == c // width, paired, 0.0).astype(jnp.bfloat16)
    a, b = iota((groups * width, rows), 0), iota((groups * width, rows), 1)
    repeated = nn(paired, bits(a % width == b % width))
    repeated = jnp.where(own_span(rows, width), repeated, 0.0).astype(jnp.bfloat16)
    notes = nn(spread(group_cap, rows), repeated)
    first = send_ref[:, 0:rows].astype(jnp.float32)
    send_ref[:, 0:rows] = (first + notes).astype(jnp.bfloat16)
    for copy in packs:
        copy.wait()


def second_kernel(group_cap, width, lane_cap, got_ref, *refs):
    out_ref, gated_ref = refs[-2:]
    rows = got_ref.shape[0]
    got = got_ref[...]
    notes = nn(collect(group_cap, rows), got[:, 0:rows])
    notes = jnp.where(own_span(rows, width), notes, 0.0).astype(jnp.bfloat16)
    slots = width * lane_cap
    a, b = iota((rows, slots), 0), iota((rows, slots), 1)
    gate = nn(notes, bits((a % width == b // lane_cap) & (a < group_cap * width)))
    hit = gate != 0.0
    rank = nn(bits(iota((rows, rows), 1) < iota((rows, rows), 0)), bits(hit))
    place = hit & (rank == (b % lane_cap).astype(jnp.float32))
    gated_ref[...] = jnp.where(place, gate, 0.0).astype(jnp.bfloat16)
    turned = jnp.transpose(jnp.where(place, 1.0, 0.0)).astype(jnp.bfloat16)
    moved = nn(turned, got).astype(jnp.bfloat16)
    for half in range(HALVES):
        out_ref[half] = moved


def partial_kernel(rows_ref, down_ref, out_ref):
    out_ref[...] = nt(rows_ref[...], down_ref[...]).astype(jnp.bfloat16)


def cycle_sum(terms):
    count = len(terms)
    while count > 1:
        count //= 2
        terms = [terms[i] + terms[i + count] for i in range(count)]
    return terms[0]


def prepare_kernel(count, preacts_ref, *refs):
    blocks = by_step(refs[:count])
    early = by_step([preacts_ref, *refs[count : 2 * count - 1]])
    weight_ref, swish_ref, slope_ref, hidden_ref = refs[2 * count - 1 :]
    columns = weight_ref.shape[0]
    slots = swish_ref.shape[0]
    for at, block_ref in enumerate(blocks):
        for part in range(2):
            first = (2 * at + part) * TILE
            weight_ref[:, first : first + TILE] = block_ref[part * columns : (part + 1) * columns, :]
    tail = early[1].shape[0] - 2 * slots
    raw = jnp.concatenate(
        [preacts_ref[...]] + [block_ref[tail:, :] for block_ref in early[1:]], axis=1
    )
    slot, row = iota((slots, 2 * slots), 0), iota((slots, 2 * slots), 1)
    gate_pre = nn(bits(row == 2 * slot), raw)
    up_pre = nn(bits(row == 2 * slot + 1), raw)
    sigmoid_value = jax.nn.sigmoid(gate_pre)
    swish_value = gate_pre * sigmoid_value
    swish_ref[...] = swish_value
    slope_ref[...] = up_pre * (sigmoid_value * (1.0 + gate_pre * (1.0 - sigmoid_value)))
    hidden_ref[...] = swish_value * up_pre


def expert_kernel(count, lane_cap, *refs):
    parts = by_step(refs[:count])
    weight_ref, swish_ref, slope_ref, hidden_ref, out_ref = refs[count:]
    slots = parts[0].shape[0]
    columns = weight_ref.shape[0]
    grads, scores = [], []
    for at in range(count):
        pieces = []
        for step in range(count):
            source = (at - step) % count
            pieces.append(
                parts[step][:, source * TILE : (source + 1) * TILE].astype(jnp.float32)
            )
        back = cycle_sum(pieces)
        lanes = slice(at * TILE, (at + 1) * TILE)
        scores.append(hidden_ref[:, lanes] * back)
        grads.append((slope_ref[:, lanes] * back).astype(jnp.bfloat16))
        grads.append((swish_ref[:, lanes] * back).astype(jnp.bfloat16))
    total = nt(jnp.concatenate(grads, axis=1), weight_ref[...]).astype(jnp.bfloat16)
    lane_count = slots // lane_cap
    pieces = [
        total[:, first : first + TILE].reshape(lane_count, lane_cap, TILE)
        for first in range(0, columns, TILE)
    ]
    score = jnp.sum(cycle_sum(scores), axis=1, keepdims=True)
    lane = lax.rem(lax.axis_index("narrow"), lane_count // HALVES)
    slot, place = iota((slots, TILE), 0), iota((slots, TILE), 1)
    score = jnp.where(place == lane * lane_cap + slot % lane_cap, score, 0.0)
    score = jnp.sum(score.reshape(lane_count, lane_cap, TILE), axis=1, keepdims=True)
    pieces.append(jnp.broadcast_to(score, (lane_count, BLOCK, TILE)).astype(jnp.bfloat16))
    out_ref[...] = jnp.concatenate(pieces, axis=1)


def rows_kernel(group_cap, width, lane_cap, gated_ref, back_ref, out_ref):
    rows, columns = out_ref.shape
    gated = gated_ref[...]
    lane_count = back_ref.shape[0]
    pieces = [
        back_ref[:, tile * lane_cap : (tile + 1) * lane_cap, :].reshape(lane_count * lane_cap, TILE)
        for tile in range(columns // TILE)
    ]
    both = jnp.concatenate([gated, gated], axis=1)
    out_ref[...] = nn(both, jnp.concatenate(pieces, axis=1)).astype(jnp.bfloat16)
    score = back_ref[...][:, columns // TILE * lane_cap :, :].astype(jnp.float32)
    score = jnp.sum(jnp.sum(score, axis=0)[0:1, :], axis=0, keepdims=True)
    score = jnp.where(gated != 0, score, 0.0).astype(jnp.bfloat16)
    a, b = iota((rows, TILE), 0), iota((rows, TILE), 1)
    score = nn(score, bits(a // lane_cap == b % width))
    score = jnp.where(own_span(rows, width), score, 0.0).astype(jnp.bfloat16)
    notes = nn(spread(group_cap, rows), score)
    first = out_ref[:, 0:rows].astype(jnp.float32)
    out_ref[:, 0:rows] = (first + notes).astype(jnp.bfloat16)


def last_kernel(group_cap, width, ids_ref, place_ref, home_ref, tokens_ref, gates_ref):
    top, tokens = ids_ref.shape
    rows = home_ref.shape[0]
    ids = ids_ref[...]
    home = home_ref[...]
    place = jnp.transpose(place_ref[...].astype(jnp.float32)).astype(jnp.bfloat16)
    tokens_ref[...] = nn(place, home).astype(jnp.bfloat16)
    notes = nn(collect(group_cap, rows), home[:, 0:rows])
    notes = jnp.where(own_span(rows, width), notes, 0.0).astype(jnp.bfloat16)
    a, b = iota((rows, rows), 0), iota((rows, rows), 1)
    wide = nn(notes, bits((a % width == b % width) & (a < group_cap * width)))
    wide = jnp.where(a // BLOCK == b // width, wide, 0.0).astype(jnp.bfloat16)
    score = jnp.transpose(nn(place, wide))
    at = iota((rows, tokens), 0)
    for k in range(top):
        gates_ref[k : k + 1, :] = jnp.sum(
            jnp.where(ids[k : k + 1, :] == at, score, 0.0), axis=0, keepdims=True
        )


def exchange(values, axis):
    return lax.all_to_all(values, axis, split_axis=0, concat_axis=0, tiled=True)


def shift(values, step, count):
    return lax.ppermute(
        values, "tp", [(source, (source + step) % count) for source in range(count)]
    )


def far_first(count):
    return [0] + sorted(range(1, count), key=lambda step: -min(step, count - step))


def by_step(values):
    order = far_first(len(values))
    return [values[order.index(step)] for step in range(len(values))]


def shift_all(values):
    count = len(values)
    return [values[0]] + [shift(values[step], step, count) for step in range(1, count)]


def per_device(d_out, expert_ids, gate_values, stored_preacts, w_gate, w_up, w_down):
    wide_count = lax.axis_size("wide")
    lane_count = lax.axis_size("narrow")
    split_count = lax.axis_size("tp")
    group_width = lane_count // HALVES
    token_count, model_width = d_out.shape
    slot_count = stored_preacts.shape[2]
    hidden_width = stored_preacts.shape[4]
    lane_cap = slot_count // lane_count
    group_cap = min(token_count, max(1, 3 * token_count * LIMIT // (2 * wide_count)))
    columns = model_width // split_count
    rows = wide_count * BLOCK
    lanes = group_width * lane_cap
    ids = expert_ids.T

    preacts = stored_preacts[0, 0].reshape(2 * slot_count, hidden_width)
    tiles = columns // TILE
    early_rows = tiles * hidden_width + 2 * slot_count
    others = split_count - 1
    send, place, *early = call(
        lambda *refs: first_kernel(group_cap, group_width, split_count, *refs),
        [shape(rows, columns), shape(rows, token_count)]
        + [shape(early_rows, hidden_width)] * others,
        (ids, gate_values.T, d_out, w_down[0, 0], preacts),
        spaces=[pltpu.HBM] * 5,
        out_spaces=[pltpu.VMEM] * (2 + others),
        vmem=60,
        scratch=[
            pltpu.VMEM(ids.shape, ids.dtype),
            pltpu.VMEM(ids.shape, gate_values.dtype),
            pltpu.VMEM((token_count, columns), d_out.dtype),
            pltpu.SemaphoreType.DMA((3 + others * (tiles + 1),)),
        ],
    )
    early = shift_all([None] + early)
    early = [early[step] for step in far_first(split_count)[1:]]
    down_cols = call(
        join_kernel,
        shape(split_count * hidden_width, columns),
        (w_down[0, 0], *early),
        size=1 << 20,
        flops=18 * 10**9,
    )

    got = exchange(send.reshape(wide_count, BLOCK, columns), "wide").reshape(rows, columns)
    forward, gated = call(
        lambda *refs: second_kernel(group_cap, group_width, lane_cap, *refs),
        [shape(HALVES, lanes, columns), shape(rows, lanes)],
        (got,),
    )
    rest_packed = call(
        pack_rest_kernel,
        [shape(2 * columns, hidden_width)] * split_count,
        (
            w_gate[0, 0],
            w_up[0, 0],
            gated,
        ),
        size=4 << 20,
        spaces=[pltpu.VMEM] * 2 + [pl.ANY],
    )
    blocks = shift_all(rest_packed)
    slot_rows = exchange(forward.reshape(lane_count, lane_cap, columns), "narrow").reshape(
        slot_count, columns
    )
    partial = call(
        partial_kernel,
        shape(slot_count, split_count * hidden_width),
        (slot_rows, down_cols),
    )
    parts = shift_all([partial] * split_count)
    hidden_all = split_count * hidden_width
    prepared = call(
        lambda *refs: prepare_kernel(split_count, *refs),
        [shape(columns, 2 * hidden_all)]
        + [shape(slot_count, hidden_all, dtype=jnp.float32)] * 3,
        (preacts, *(blocks[step] for step in far_first(split_count)), *early),
        size=8 << 20,
    )
    block_rows = columns // TILE * lane_cap + BLOCK
    terms = call(
        lambda *refs: expert_kernel(split_count, lane_cap, *refs),
        shape(lane_count, block_rows, TILE),
        (*(parts[step] for step in far_first(split_count)), *prepared),
        vmem=24,
    )
    back = exchange(terms, "narrow")
    row_input = call(
        lambda *refs: rows_kernel(group_cap, group_width, lane_cap, *refs),
        shape(rows, columns),
        (gated, back),
    )
    home = exchange(row_input.reshape(wide_count, BLOCK, columns), "wide").reshape(rows, columns)
    d_tokens, d_gates = call(
        lambda *refs: last_kernel(group_cap, group_width, *refs),
        [
            shape(token_count, columns),
            shape(expert_ids.shape[1], token_count, dtype=jnp.float32),
        ],
        (ids, place, home),
    )
    return (d_tokens, d_gates.T)


def solution(mesh):
    return jax.shard_map(
        per_device,
        mesh=mesh,
        in_specs=(
            P(("wide", "narrow"), None),
            P(("wide", "narrow"), None),
            P(("wide", "narrow"), None),
            P("wide", "narrow", None, None, "tp"),
            P("wide", "narrow", None, "tp"),
            P("wide", "narrow", None, "tp"),
            P("wide", "narrow", "tp", None),
        ),
        out_specs=(P(("wide", "narrow"), "tp"), P(("wide", "narrow"), None)),
        check_vma=False,
    )
```

```python
import jax
import jax.numpy as jnp
from jax import lax
from jax.experimental import pallas as pl
from jax.experimental.pallas import tpu as pltpu
from jax.sharding import PartitionSpec as P

LIMIT = 4
HALVES = 2
BLOCK = 8
TILE = 128


def nn(left, right):
    return lax.dot_general(
        left, right, (((1,), (0,)), ((), ())), preferred_element_type=jnp.float32
    )


def nt(left, right):
    return lax.dot_general(
        left, right, (((1,), (1,)), ((), ())), preferred_element_type=jnp.float32
    )


def iota(shape, axis):
    return lax.broadcasted_iota(jnp.int32, shape, axis)


def bits(mask):
    return jnp.where(mask, 1.0, 0.0).astype(jnp.bfloat16)


def call(kernel, outs, args, flops=0, size=1 << 20, spaces=None, out_spaces=None, scratch=(), vmem=16):
    spaces = spaces or [pltpu.VMEM] * len(args)
    return pl.pallas_call(
        kernel,
        out_shape=outs,
        in_specs=[pl.BlockSpec(memory_space=space) for space in spaces],
        out_specs=[pl.BlockSpec(memory_space=space) for space in out_spaces]
        if out_spaces
        else jax.tree.map(lambda _: pl.BlockSpec(memory_space=pltpu.VMEM), outs),
        scratch_shapes=list(scratch),
        compiler_params=pltpu.CompilerParams(vmem_limit_bytes=vmem << 20),
        cost_estimate=pl.CostEstimate(flops=flops, bytes_accessed=size, transcendentals=0),
    )(*args)


def shape(*dims, dtype=jnp.bfloat16):
    return jax.ShapeDtypeStruct(dims, dtype)


def pack_rest_kernel(gate_ref, up_ref, after_ref, *out_refs):
    count = len(out_refs) + 1
    width = gate_ref.shape[0] // count
    me = lax.axis_index("tp")
    for step, out_ref in enumerate(out_refs, 1):
        to = lax.rem(me + step, count)
        rows = pl.ds(pl.multiple_of(to * width, TILE), width)
        out_ref[0:width, :] = gate_ref[rows, :]
        out_ref[width : 2 * width, :] = up_ref[rows, :]


def join_kernel(down_ref, *refs):
    block_refs, out_ref = by_step([down_ref, *refs[:-1]])[1:], refs[-1]
    hidden, columns = down_ref.shape[0], out_ref.shape[1]
    own = lax.axis_index("tp") * columns
    out_ref[0:hidden, :] = down_ref[:, pl.ds(pl.multiple_of(own, TILE), columns)]
    for at, block_ref in enumerate(block_refs, 1):
        for tile in range(columns // TILE):
            out_ref[at * hidden : (at + 1) * hidden, tile * TILE : (tile + 1) * TILE] = (
                block_ref[tile * hidden : (tile + 1) * hidden, :]
            )


def spread(group_cap, rows):
    r, c = iota((rows, rows), 0), iota((rows, rows), 1)
    return bits((r // BLOCK == c // BLOCK) & (r % BLOCK == group_cap))


def collect(group_cap, rows):
    r, c = iota((rows, rows), 0), iota((rows, rows), 1)
    return bits(
        (r // BLOCK == c // BLOCK) & (c % BLOCK == group_cap) & (r % BLOCK < group_cap)
    )


def own_span(rows, width):
    r, c = iota((rows, rows), 0), iota((rows, rows), 1)
    return c // width == r % BLOCK


def first_kernel(
    group_cap, width, count, ids_hbm, gates_hbm, rows_hbm, down_hbm, preacts_hbm, *refs
):
    send_ref, place_ref = refs[:2]
    block_refs = refs[2 : 1 + count]
    ids_ref, gates_ref, rows_ref, sems = refs[1 + count :]
    columns = send_ref.shape[1]
    me = lax.axis_index("tp")

    def columns_of(index):
        return pl.ds(pl.multiple_of(index * columns, TILE), columns)

    loads = [
        pltpu.make_async_copy(ids_hbm, ids_ref, sems.at[0]),
        pltpu.make_async_copy(gates_hbm, gates_ref, sems.at[1]),
        pltpu.make_async_copy(rows_hbm.at[:, columns_of(me)], rows_ref, sems.at[2]),
    ]
    packs = []
    hidden = down_hbm.shape[0]
    for step, block_ref in enumerate(block_refs, 1):
        first = lax.rem(me + step, count) * columns
        for tile in range(columns // TILE):
            lanes = pl.ds(pl.multiple_of(first + tile * TILE, TILE), TILE)
            packs.append((down_hbm.at[:, lanes], block_ref.at[pl.ds(tile * hidden, hidden)]))
        tail = pl.ds(columns // TILE * hidden, preacts_hbm.shape[0])
        packs.append((preacts_hbm, block_ref.at[tail]))
    packs = [
        pltpu.make_async_copy(source, target, sems.at[3 + at])
        for at, (source, target) in enumerate(packs)
    ]
    for copy in loads + packs:
        copy.start()
    for copy in loads:
        copy.wait()
    top, tokens = ids_ref.shape
    rows = send_ref.shape[0]
    groups = rows // BLOCK
    ids = ids_ref[...]
    gates = gates_ref[...].astype(jnp.float32)
    member = jnp.zeros((groups, tokens), jnp.float32)
    table = jnp.zeros((groups * width, tokens), jnp.float32)
    for k in range(top):
        one = ids[k : k + 1, :]
        member = jnp.where(one // width == iota((groups, tokens), 0), 1.0, member)
        table = jnp.where(one == iota((groups * width, tokens), 0), gates[k : k + 1, :], table)
    earlier = bits(iota((tokens, tokens), 0) < iota((tokens, tokens), 1))
    rank = nn(member.astype(jnp.bfloat16), earlier)
    rank = jnp.where((member > 0) & (rank < group_cap), rank, 100.0)
    grow = bits(iota((rows, groups), 0) // BLOCK == iota((rows, groups), 1))
    place = nn(grow, rank.astype(jnp.bfloat16)) == (
        iota((rows, tokens), 0) % BLOCK
    ).astype(jnp.float32)
    place = bits(place)
    place_ref[...] = place
    send_ref[...] = nn(place, rows_ref[...]).astype(jnp.bfloat16)
    r, c = iota((rows, groups * width), 0), iota((rows, groups * width), 1)
    paired = nt(place, table.astype(jnp.bfloat16))
    paired = jnp.where(r // BLOCK == c // width, paired, 0.0).astype(jnp.bfloat16)
    a, b = iota((groups * width, rows), 0), iota((groups * width, rows), 1)
    repeated = nn(paired, bits(a % width == b % width))
    repeated = jnp.where(own_span(rows, width), repeated, 0.0).astype(jnp.bfloat16)
    notes = nn(spread(group_cap, rows), repeated)
    first = send_ref[:, 0:rows].astype(jnp.float32)
    send_ref[:, 0:rows] = (first + notes).astype(jnp.bfloat16)
    for copy in packs:
        copy.wait()


def second_kernel(group_cap, width, lane_cap, got_ref, *refs):
    out_ref, gated_ref = refs[-2:]
    rows = got_ref.shape[0]
    got = got_ref[...]
    notes = nn(collect(group_cap, rows), got[:, 0:rows])
    notes = jnp.where(own_span(rows, width), notes, 0.0).astype(jnp.bfloat16)
    slots = width * lane_cap
    a, b = iota((rows, slots), 0), iota((rows, slots), 1)
    gate = nn(notes, bits((a % width == b // lane_cap) & (a < group_cap * width)))
    hit = gate != 0.0
    rank = nn(bits(iota((rows, rows), 1) < iota((rows, rows), 0)), bits(hit))
    place = hit & (rank == (b % lane_cap).astype(jnp.float32))
    gated_ref[...] = jnp.where(place, gate, 0.0).astype(jnp.bfloat16)
    turned = jnp.transpose(jnp.where(place, 1.0, 0.0)).astype(jnp.bfloat16)
    moved = nn(turned, got).astype(jnp.bfloat16)
    for half in range(HALVES):
        out_ref[half] = moved


def partial_kernel(rows_ref, down_ref, out_ref):
    out_ref[...] = nt(rows_ref[...], down_ref[...]).astype(jnp.bfloat16)


def cycle_sum(terms):
    count = len(terms)
    while count > 1:
        count //= 2
        terms = [terms[i] + terms[i + count] for i in range(count)]
    return terms[0]


def prepare_kernel(count, preacts_ref, gate_hbm, up_hbm, *refs):
    blocks = by_step([None, *refs[: count - 1]])
    early = by_step([preacts_ref, *refs[count - 1 : 2 * count - 2]])
    weight_ref, swish_ref, slope_ref, hidden_ref, own_ref, sems = refs[2 * count - 2 :]
    columns = weight_ref.shape[0]
    slots = swish_ref.shape[0]
    own = pl.ds(pl.multiple_of(lax.axis_index("tp") * columns, TILE), columns)
    copies = [
        pltpu.make_async_copy(source.at[own], own_ref.at[part], sems.at[part])
        for part, source in enumerate((gate_hbm, up_hbm))
    ]
    for copy in copies:
        copy.start()
    for at, block_ref in enumerate(blocks[1:], 1):
        for part in range(2):
            first = (2 * at + part) * TILE
            weight_ref[:, first : first + TILE] = block_ref[part * columns : (part + 1) * columns, :]
    tail = early[1].shape[0] - 2 * slots
    raw = jnp.concatenate(
        [preacts_ref[...]] + [block_ref[tail:, :] for block_ref in early[1:]], axis=1
    )
    slot, row = iota((slots, 2 * slots), 0), iota((slots, 2 * slots), 1)
    gate_pre = nn(bits(row == 2 * slot), raw)
    up_pre = nn(bits(row == 2 * slot + 1), raw)
    sigmoid_value = jax.nn.sigmoid(gate_pre)
    swish_value = gate_pre * sigmoid_value
    swish_ref[...] = swish_value
    slope_ref[...] = up_pre * (sigmoid_value * (1.0 + gate_pre * (1.0 - sigmoid_value)))
    hidden_ref[...] = swish_value * up_pre
    for part, copy in enumerate(copies):
        copy.wait()
        weight_ref[:, part * TILE : (part + 1) * TILE] = own_ref[part]


def expert_kernel(count, lane_cap, *refs):
    parts = by_step(refs[:count])
    weight_ref, swish_ref, slope_ref, hidden_ref, out_ref = refs[count:]
    slots = parts[0].shape[0]
    columns = weight_ref.shape[0]
    grads, scores = [], []
    for at in range(count):
        pieces = []
        for step in range(count):
            source = (at - step) % count
            pieces.append(
                parts[step][:, source * TILE : (source + 1) * TILE].astype(jnp.float32)
            )
        back = cycle_sum(pieces)
        lanes = slice(at * TILE, (at + 1) * TILE)
        scores.append(hidden_ref[:, lanes] * back)
        grads.append((slope_ref[:, lanes] * back).astype(jnp.bfloat16))
        grads.append((swish_ref[:, lanes] * back).astype(jnp.bfloat16))
    total = nt(jnp.concatenate(grads, axis=1), weight_ref[...]).astype(jnp.bfloat16)
    lane_count = slots // lane_cap
    pieces = [
        total[:, first : first + TILE].reshape(lane_count, lane_cap, TILE)
        for first in range(0, columns, TILE)
    ]
    score = jnp.sum(cycle_sum(scores), axis=1, keepdims=True)
    lane = lax.rem(lax.axis_index("narrow"), lane_count // HALVES)
    slot, place = iota((slots, TILE), 0), iota((slots, TILE), 1)
    score = jnp.where(place == lane * lane_cap + slot % lane_cap, score, 0.0)
    score = jnp.sum(score.reshape(lane_count, lane_cap, TILE), axis=1, keepdims=True)
    pieces.append(jnp.broadcast_to(score, (lane_count, BLOCK, TILE)).astype(jnp.bfloat16))
    out_ref[...] = jnp.concatenate(pieces, axis=1)


def rows_kernel(group_cap, width, lane_cap, gated_ref, back_ref, out_ref):
    rows, columns = out_ref.shape
    gated = gated_ref[...]
    lane_count = back_ref.shape[0]
    pieces = [
        back_ref[:, tile * lane_cap : (tile + 1) * lane_cap, :].reshape(lane_count * lane_cap, TILE)
        for tile in range(columns // TILE)
    ]
    both = jnp.concatenate([gated, gated], axis=1)
    out_ref[...] = nn(both, jnp.concatenate(pieces, axis=1)).astype(jnp.bfloat16)
    score = back_ref[...][:, columns // TILE * lane_cap :, :].astype(jnp.float32)
    score = jnp.sum(jnp.sum(score, axis=0)[0:1, :], axis=0, keepdims=True)
    score = jnp.where(gated != 0, score, 0.0).astype(jnp.bfloat16)
    a, b = iota((rows, TILE), 0), iota((rows, TILE), 1)
    score = nn(score, bits(a // lane_cap == b % width))
    score = jnp.where(own_span(rows, width), score, 0.0).astype(jnp.bfloat16)
    notes = nn(spread(group_cap, rows), score)
    first = out_ref[:, 0:rows].astype(jnp.float32)
    out_ref[:, 0:rows] = (first + notes).astype(jnp.bfloat16)


def last_kernel(group_cap, width, ids_ref, place_ref, home_ref, tokens_ref, gates_ref):
    top, tokens = ids_ref.shape
    rows = home_ref.shape[0]
    ids = ids_ref[...]
    home = home_ref[...]
    place = jnp.transpose(place_ref[...].astype(jnp.float32)).astype(jnp.bfloat16)
    tokens_ref[...] = nn(place, home).astype(jnp.bfloat16)
    notes = nn(collect(group_cap, rows), home[:, 0:rows])
    notes = jnp.where(own_span(rows, width), notes, 0.0).astype(jnp.bfloat16)
    a, b = iota((rows, rows), 0), iota((rows, rows), 1)
    wide = nn(notes, bits((a % width == b % width) & (a < group_cap * width)))
    wide = jnp.where(a // BLOCK == b // width, wide, 0.0).astype(jnp.bfloat16)
    score = jnp.transpose(nn(place, wide))
    at = iota((rows, tokens), 0)
    for k in range(top):
        gates_ref[k : k + 1, :] = jnp.sum(
            jnp.where(ids[k : k + 1, :] == at, score, 0.0), axis=0, keepdims=True
        )


def exchange(values, axis):
    return lax.all_to_all(values, axis, split_axis=0, concat_axis=0, tiled=True)


def shift(values, step, count):
    return lax.ppermute(
        values, "tp", [(source, (source + step) % count) for source in range(count)]
    )


def far_first(count):
    return [0] + sorted(range(1, count), key=lambda step: -min(step, count - step))


def by_step(values):
    order = far_first(len(values))
    return [values[order.index(step)] for step in range(len(values))]


def shift_all(values):
    count = len(values)
    return [values[0]] + [shift(values[step], step, count) for step in range(1, count)]


def per_device(d_out, expert_ids, gate_values, stored_preacts, w_gate, w_up, w_down):
    wide_count = lax.axis_size("wide")
    lane_count = lax.axis_size("narrow")
    split_count = lax.axis_size("tp")
    group_width = lane_count // HALVES
    token_count, model_width = d_out.shape
    slot_count = stored_preacts.shape[2]
    hidden_width = stored_preacts.shape[4]
    lane_cap = slot_count // lane_count
    group_cap = min(token_count, max(1, 3 * token_count * LIMIT // (2 * wide_count)))
    columns = model_width // split_count
    rows = wide_count * BLOCK
    lanes = group_width * lane_cap
    ids = expert_ids.T

    preacts = stored_preacts[0, 0].reshape(2 * slot_count, hidden_width)
    tiles = columns // TILE
    early_rows = tiles * hidden_width + 2 * slot_count
    others = split_count - 1
    send, place, *early = call(
        lambda *refs: first_kernel(group_cap, group_width, split_count, *refs),
        [shape(rows, columns), shape(rows, token_count)]
        + [shape(early_rows, hidden_width)] * others,
        (ids, gate_values.T, d_out, w_down[0, 0], preacts),
        spaces=[pltpu.HBM] * 5,
        out_spaces=[pltpu.VMEM] * (2 + others),
        vmem=60,
        scratch=[
            pltpu.VMEM(ids.shape, ids.dtype),
            pltpu.VMEM(ids.shape, gate_values.dtype),
            pltpu.VMEM((token_count, columns), d_out.dtype),
            pltpu.SemaphoreType.DMA((3 + others * (tiles + 1),)),
        ],
    )
    early = shift_all([None] + early)
    early = [early[step] for step in far_first(split_count)[1:]]
    down_cols = call(
        join_kernel,
        shape(split_count * hidden_width, columns),
        (w_down[0, 0], *early),
        size=1 << 20,
        flops=18 * 10**9,
    )

    got = exchange(send.reshape(wide_count, BLOCK, columns), "wide").reshape(rows, columns)
    forward, gated = call(
        lambda *refs: second_kernel(group_cap, group_width, lane_cap, *refs),
        [shape(HALVES, lanes, columns), shape(rows, lanes)],
        (got,),
    )
    rest_packed = call(
        pack_rest_kernel,
        [shape(2 * columns, hidden_width)] * others,
        (
            w_gate[0, 0],
            w_up[0, 0],
            gated,
        ),
        size=4 << 20,
        spaces=[pltpu.VMEM] * 2 + [pl.ANY],
    )
    blocks = shift_all([None, *rest_packed])
    slot_rows = exchange(forward.reshape(lane_count, lane_cap, columns), "narrow").reshape(
        slot_count, columns
    )
    partial = call(
        partial_kernel,
        shape(slot_count, split_count * hidden_width),
        (slot_rows, down_cols),
    )
    parts = shift_all([partial] * split_count)
    hidden_all = split_count * hidden_width
    prepared = call(
        lambda *refs: prepare_kernel(split_count, *refs),
        [shape(columns, 2 * hidden_all)]
        + [shape(slot_count, hidden_all, dtype=jnp.float32)] * 3,
        (
            preacts,
            w_gate[0, 0],
            w_up[0, 0],
            *(blocks[step] for step in far_first(split_count)[1:]),
            *early,
        ),
        spaces=[pltpu.VMEM] + [pl.ANY] * 2 + [pltpu.VMEM] * (2 * others),
        scratch=[
            pltpu.VMEM((2, columns, hidden_width), w_gate.dtype),
            pltpu.SemaphoreType.DMA((2,)),
        ],
        size=8 << 20,
    )
    block_rows = columns // TILE * lane_cap + BLOCK
    terms = call(
        lambda *refs: expert_kernel(split_count, lane_cap, *refs),
        shape(lane_count, block_rows, TILE),
        (*(parts[step] for step in far_first(split_count)), *prepared),
        vmem=24,
    )
    back = exchange(terms, "narrow")
    row_input = call(
        lambda *refs: rows_kernel(group_cap, group_width, lane_cap, *refs),
        shape(rows, columns),
        (gated, back),
    )
    home = exchange(row_input.reshape(wide_count, BLOCK, columns), "wide").reshape(rows, columns)
    d_tokens, d_gates = call(
        lambda *refs: last_kernel(group_cap, group_width, *refs),
        [
            shape(token_count, columns),
            shape(expert_ids.shape[1], token_count, dtype=jnp.float32),
        ],
        (ids, place, home),
    )
    return (d_tokens, d_gates.T)


def solution(mesh):
    return jax.shard_map(
        per_device,
        mesh=mesh,
        in_specs=(
            P(("wide", "narrow"), None),
            P(("wide", "narrow"), None),
            P(("wide", "narrow"), None),
            P("wide", "narrow", None, None, "tp"),
            P("wide", "narrow", None, "tp"),
            P("wide", "narrow", None, "tp"),
            P("wide", "narrow", "tp", None),
        ),
        out_specs=(P(("wide", "narrow"), "tp"), P(("wide", "narrow"), None)),
        check_vma=False,
    )
```
